512 devices in a mesh: ifg: 32 (over x, z_hi, core), band: 16 (over z_lo, y).
Axes of the slice: x: 4, y: 8, z: 8 (z_hi: 4, z_lo: 2; z = z_hi * 2 + z_lo), core: 2. Of those that a mesh axis runs over, the one named last changes fastest.
Arguments:
- unwrapped: float32 [1536, 96, 1536], P('ifg', 'band'), may hold values from -6 to 6
- component_mask: int32 [1536, 96, 1536], P('ifg', 'band'), may hold values 0 or 1
- date_pairs: int32 [1536, 2], replicated, may hold values from 0 to 299, as said below
Outputs:
- series: float32 [300, 96, 1536], P(None, 'band', 'ifg')
- corrected: float32 [300, 96, 1536], P(None, 'band', 'ifg')
The draws below stay inside these ranges and needn't reach their ends.
Inputs may be any that keep to these rules, and one draw needn't show every extreme that they name: `date_pairs`: in each row the first date is earlier than the second and at most 40 dates before it.
All inputs are finite; a program needn't handle non-finite values. No bound on the sum of `component_mask` on one device may be relied on, other than what follows from the above.
Results may differ from the reference program's by a relative error of at most 0.00007.
Values sent between devices are 32-bit elements; how exact they have to be, the bound alone decides.
No kernel may reach another device: no remote copies, remote signals or barrier semaphores. Data moves between devices by JAX's collectives and lax.ppermute only.
A program may use at most 64 MiB of HBM per device.

```python
import jax
import jax.numpy as jnp
from jax import lax

DATES = 300
IFGS = 1536
ROWS = 96
COLS = 1536
SPAN = 40
TIME_SIGMA = 6
RIM_WIDTH = 4


def draw_date_pairs(key, part):
    key = jax.random.fold_in(key, 11)
    first_key = jax.random.fold_in(key, 1)
    step_key = jax.random.fold_in(key, 2)
    position = jnp.arange(IFGS, dtype=jnp.int32)
    earlier = jax.random.randint(first_key, (IFGS,), 0, DATES - 1, dtype=jnp.int32)
    earlier = jnp.where(position == 0, 0, earlier)
    earlier = jnp.where(position == IFGS - 1, DATES - 2, earlier)
    stride = jax.random.randint(step_key, (IFGS,), 1, SPAN + 1, dtype=jnp.int32)
    later = jnp.minimum(earlier + stride, DATES - 1)
    return jnp.stack([earlier, later], axis=1)


def place_ends(values, rng, least, largest):
    index_at = [jax.random.randint(jax.random.fold_in(rng, axis), (), 0, length) for axis, length in enumerate(values.shape)]
    widest = values.shape.index(max(values.shape))
    neighbour = index_at[:widest] + [(index_at[widest] + 1) % values.shape[widest]] + index_at[widest + 1:]
    return values.at[tuple(index_at)].set(least).at[tuple(neighbour)].set(largest)


def steps_of(rng, dims, cuts, low, largest):
    factor_of, own = 1.0, jax.random.fold_in(rng, 6)
    for dim, blocks in cuts:
        steps = jnp.exp(jax.random.uniform(jax.random.fold_in(own, dim), (blocks,), jnp.float32, low / len(cuts), largest / len(cuts)))
        factor_of = factor_of * jnp.repeat(steps, dims[dim] // blocks).reshape([-1 if axis == dim else 1 for axis in range(len(dims))])
    return factor_of


def normal_values(stream_key, shape, scale, reach, cuts=(), kind=jnp.bfloat16):
    array = jax.random.normal(stream_key, shape, jnp.float32) * scale
    if len(cuts) > 0:
        array = steps_of(stream_key, shape, cuts, -0.22, 0.18) * array
    return jnp.clip(array, min=-reach, max=reach).astype(kind)


def setup_inputs(seed: int = 0) -> dict:
    key_of = jax.random.split(jax.random.key(seed), 4)
    return {
        "unwrapped": normal_values(key_of[0], (IFGS, ROWS, COLS), 1.0, 6.0, ((0, 32), (1, 16)), jnp.float32),
        "component_mask": place_ends((jax.random.randint(key_of[1], (IFGS, ROWS, COLS), 0, 8) < 7).astype(jnp.int32), jax.random.fold_in(key_of[1], 1), 0, 1),
        "date_pairs": draw_date_pairs(jax.random.fold_in(key_of[3], 71), 0),
    }


def pseudo_inverse(date_pairs, num_dates):
    calendar = jnp.arange(num_dates, dtype=jnp.int32)
    design = (date_pairs[:, 1:2] == calendar[None, :]).astype(jnp.float32) - (date_pairs[:, 0:1] == calendar[None, :]).astype(jnp.float32)
    normal = jnp.dot(design.T, design, precision=lax.Precision.HIGHEST) + jnp.eye(num_dates, dtype=jnp.float32)
    factor = jnp.linalg.cholesky(normal)
    return jax.scipy.linalg.cho_solve((factor, True), design.T)

def temporal_highpass(num_dates, sigma):
    offsets = jnp.arange(num_dates, dtype=jnp.int32).astype(jnp.float32)
    spread = offsets[:, None] - offsets[None, :]
    weights = jnp.exp(-spread * spread / (2.0 * sigma * sigma))
    return jnp.eye(num_dates, dtype=jnp.float32) - weights / jnp.sum(weights, axis=1, keepdims=True)

def spatial_taps(width):
    offsets = jnp.arange(-width, width + 1, dtype=jnp.int32).astype(jnp.float32)
    sigma = width / 2.0
    return jnp.exp(-offsets * offsets / (2.0 * sigma * sigma))

def edge_weights(start, count, total, width):
    taps = spatial_taps(width)
    places = start + jnp.arange(count, dtype=jnp.int32)[:, None] + jnp.arange(-width, width + 1, dtype=jnp.int32)[None, :]
    inside = ((places >= 0) & (places < total)).astype(jnp.float32)
    return jnp.sum(inside * taps[None, :], axis=1)

def reference(unwrapped, component_mask, date_pairs):
    inverse = pseudo_inverse(date_pairs, DATES)
    highpass = temporal_highpass(DATES, TIME_SIGMA)
    masked = unwrapped * component_mask.astype(jnp.float32)
    flat = masked.reshape(IFGS, ROWS * COLS)
    series_flat = jnp.dot(inverse, flat, precision=lax.Precision.HIGHEST)
    varying = jnp.dot(highpass, series_flat, precision=lax.Precision.HIGHEST).reshape(DATES, ROWS, COLS)
    series = series_flat.reshape(DATES, ROWS, COLS)
    taps = spatial_taps(RIM_WIDTH)
    padded = jnp.pad(varying, ((0, 0), (RIM_WIDTH, RIM_WIDTH), (0, 0)))
    rowpass = jnp.zeros((DATES, ROWS, COLS), jnp.float32)
    for offset in range(2 * RIM_WIDTH + 1):
        rowpass = rowpass + taps[offset] * padded[:, offset:offset + ROWS, :]
    rowpass = rowpass / edge_weights(0, ROWS, ROWS, RIM_WIDTH)[None, :, None]
    padded = jnp.pad(rowpass, ((0, 0), (0, 0), (RIM_WIDTH, RIM_WIDTH)))
    atmosphere = jnp.zeros((DATES, ROWS, COLS), jnp.float32)
    for offset in range(2 * RIM_WIDTH + 1):
        atmosphere = atmosphere + taps[offset] * padded[:, :, offset:offset + COLS]
    atmosphere = atmosphere / edge_weights(0, COLS, COLS, RIM_WIDTH)[None, None, :]
    return (series, series - atmosphere)
```

```python
import jax
import jax.numpy as jnp
import numpy as np
from jax import lax
from jax.experimental import pallas as pl
from jax.experimental.pallas import tpu as pltpu
from jax.sharding import PartitionSpec as P

DATES = 300
SPAN = 40
TIME_SIGMA = 6
RIM_WIDTH = 4

DATE_ROWS = 304
DATE_LANES = 384

IFG_COUNT = 32
BAND_COUNT = 16
OWN_IFGS = 48
ROWS = 6
COLS = 48
PIXELS = ROWS * COLS
IFGS = IFG_COUNT * OWN_IFGS

GROUP = 16
GROUPS = OWN_IFGS // GROUP
TAIL = PIXELS - 256
BLOCK = 2 * OWN_IFGS + GROUP
SEND_GROUP = 8
SEND_COLS = SEND_GROUP * COLS

HALO = 512
MIB = 1024 * 1024


def split(value):
    high = value.astype(jnp.bfloat16)
    low = (value - high.astype(jnp.float32)).astype(jnp.bfloat16)
    return high, low


def dot(a, b):
    return jnp.dot(a, b, preferred_element_type=jnp.float32)


def dot_split(a_high, a_low, b_high, b_low):
    return dot(a_high, b_high) + (dot(a_high, b_low) + dot(a_low, b_high))


def pieces(source, target, length):
    while length > 0:
        step = min(length, 128 - source % 128, 128 - target % 128)
        yield source // 128, target // 128, (target - source) % 128, target % 128, target % 128 + step
        source, target, length = source + step, target + step, length - step


def shifted(value, shift):
    return value if shift == 0 else pltpu.roll(value, shift, 1)


def pack_kernel(unwrapped_ref, mask_ref, out_ref):
    lane = lax.broadcasted_iota(jnp.int32, (OWN_IFGS, 128), 1)
    tail_lane = lax.broadcasted_iota(jnp.int32, (GROUP, 128), 1)
    tiles = {}
    for row in range(ROWS):
        for tile in range(SEND_COLS // 128):
            at = (row, slice(None), slice(128 * tile, 128 * tile + 128))
            tiles[row, tile] = unwrapped_ref[at] * mask_ref[at].astype(jnp.float32)
    for dest in range(SEND_GROUP):
        out = [jnp.zeros((OWN_IFGS, 128), jnp.float32) for _ in range(2)]
        tail = jnp.zeros((GROUP, 128), jnp.float32)
        for row in range(ROWS):
            start, target = dest * COLS, row * COLS
            length = min(COLS, 256 - target)
            for source_tile, tile, shift, first, last in pieces(start, target, length):
                moved = shifted(tiles[row, source_tile], shift)
                out[tile] = jnp.where((lane >= first) & (lane < last), moved, out[tile])
            if length < COLS:
                for group in range(GROUPS):
                    for source_tile, _, shift, first, last in pieces(start + length, TAIL * group, COLS - length):
                        moved = shifted(tiles[row, source_tile][GROUP * group : GROUP * (group + 1)], shift)
                        tail = jnp.where((tail_lane >= first) & (tail_lane < last), moved, tail)
        out_ref[dest, 0:OWN_IFGS, :] = out[0]
        out_ref[dest, OWN_IFGS : 2 * OWN_IFGS, :] = out[1]
        out_ref[dest, 2 * OWN_IFGS :, :] = tail


def pack(unwrapped, component_mask):
    block = pl.BlockSpec((ROWS, OWN_IFGS, SEND_COLS), lambda i: (0, 0, i))
    return pl.pallas_call(
        pack_kernel,
        grid=(IFG_COUNT // SEND_GROUP,),
        in_specs=[block, block],
        out_specs=pl.BlockSpec((SEND_GROUP, BLOCK, 128), lambda i: (i, 0, 0)),
        out_shape=jax.ShapeDtypeStruct((IFG_COUNT, BLOCK, 128), jnp.float32),
        compiler_params=pltpu.CompilerParams(vmem_limit_bytes=16 * MIB),
        cost_estimate=pl.CostEstimate(flops=2_000_000, bytes_accessed=5_400_000, transcendentals=0),
        name="mask_pack",
    )(unwrapped, component_mask)


def iota(shape, dim):
    return lax.broadcasted_iota(jnp.int32, shape, dim)


def one_hot(pairs):
    date = iota((DATE_LANES, pairs.shape[1]), 0)
    later = jnp.where(pairs[1:2, :] == date, 1.0, 0.0)
    return (later - jnp.where(pairs[0:1, :] == date, 1.0, 0.0)).astype(jnp.bfloat16)


def identity(rows, cols, first=0):
    return jnp.where(iota((rows, cols), 0) + first == iota((rows, cols), 1), 1.0, 0.0)


def eliminate(normal_ref, band_ref, lower_ref, scaled_ref):
    window = SPAN // 8 + 1
    blocks = DATE_ROWS // 8
    for tile in range(window, window + blocks):
        start = 8 * tile - SPAN
        rows = normal_ref[8 * tile : 8 * tile + 8, :]
        band_ref[8 * tile : 8 * tile + 8, :] = pltpu.roll(rows, (DATE_LANES - start) % DATE_LANES, 1)[:, :128]
    sub = iota((8, 128), 0)
    lane = iota((8, 128), 1)

    def block_step(block, carry):
        left, right = list(carry[:window]), list(carry[window:])
        pivots = jnp.zeros((8, 128), jnp.float32)
        for j in range(8):
            pivot_row = left[0][j : j + 1, :]
            right_row = right[0][j : j + 1, :]
            scale = jnp.broadcast_to(1.0 / pivot_row[:, j : j + 1], (8, 128))
            pivots = jnp.where(sub == j, scale, pivots)
            scaled_row = pivot_row * scale[0:1, :]
            scaled_right = right_row * jnp.concatenate([scale[0:1, :]] * 3, axis=1)
            for q in range(window):
                factor = jnp.broadcast_to(left[q][:, j : j + 1], (8, 128))
                if q == 0:
                    factor = jnp.where(sub > j, factor, 0.0)
                left[q] = left[q] - factor * scaled_row
                right[q] = right[q] - jnp.concatenate([factor] * 3, axis=1) * scaled_right
        at = pl.ds(pl.multiple_of(8 * block, 8), 8)
        lower_ref[at, :] = right[0]
        scaled_ref[at, :] = right[0] * jnp.concatenate([pivots] * 3, axis=1)
        entering = pl.multiple_of(8 * (block + window), 8)
        left = [jnp.where(lane < 120, pltpu.roll(part, 120, 1), 0.0) for part in left[1:]]
        left.append(band_ref[pl.ds(entering, 8), :])
        right = right[1:] + [identity(8, DATE_LANES, entering)]
        return tuple(left + right)

    left = [normal_ref[8 * q : 8 * q + 8, 0:128] for q in range(window)]
    right = [identity(8, DATE_LANES, 8 * q) for q in range(window)]
    lax.fori_loop(0, blocks, block_step, tuple(left + right))


def highpass_matrix():
    row, col = iota((DATE_ROWS, DATE_LANES), 0), iota((DATE_ROWS, DATE_LANES), 1)
    spread = (row - col).astype(jnp.float32)
    weights = jnp.exp(-spread * spread / (2.0 * TIME_SIGMA * TIME_SIGMA))
    weights = jnp.where(col < DATES, weights, 0.0)
    lowpass = weights / jnp.sum(weights, axis=1, keepdims=True)
    return jnp.where((row < DATES) & (col < DATES), identity(DATE_ROWS, DATE_LANES) - lowpass, 0.0)


def tap(offset):
    sigma = RIM_WIDTH / 2.0
    return jnp.where(jnp.abs(offset) <= RIM_WIDTH, jnp.exp(-offset * offset / (2.0 * sigma * sigma)), 0.0)


def operators_kernel(pairs_ref, ordered_ref, target_ref, source_ref, inv_high, inv_low, high_high, high_low,
                     filter_high, filter_low, normal_ref, band_ref, lower_ref, scaled_ref):
    design = one_hot(pairs_ref[...])
    normal = lax.dot_general(design, design, (((1,), (1,)), ((), ())), preferred_element_type=jnp.float32)
    normal_ref[...] = normal + identity(DATE_LANES, DATE_LANES)
    eliminate(normal_ref, band_ref, lower_ref, scaled_ref)
    solve = lax.dot_general(lower_ref[...], scaled_ref[...], (((0,), (0,)), ((), ())),
                            precision=lax.Precision.HIGHEST, preferred_element_type=jnp.float32)
    filtered = jnp.dot(highpass_matrix(), solve, precision=lax.Precision.HIGHEST, preferred_element_type=jnp.float32)
    for matrix, high_ref, low_ref in ((solve[:DATE_ROWS], inv_high, inv_low), (filtered, high_high, high_low)):
        first, second = split(matrix)
        third = (matrix - first.astype(jnp.float32) - second.astype(jnp.float32)).astype(jnp.bfloat16)
        for group in range(GROUPS):
            at = slice(512 * group, 512 * group + 512)
            ordered = one_hot(ordered_ref[:, at])
            product = dot(first, ordered) + (dot(second, ordered) + dot(third, ordered))
            high_ref[:, at], low_ref[:, at] = split(product)
    weights = tap(source_ref[0:1, :] - target_ref[:, 0:1]) * tap(source_ref[1:2, :] - target_ref[:, 1:2])
    filter_high[...], filter_low[...] = split(weights / target_ref[:, 2:3])


def operators(date_pairs, norm):
    pairs = date_pairs.T
    ordered = pairs.reshape(2, IFG_COUNT, GROUPS, GROUP).transpose(0, 2, 1, 3).reshape(2, IFGS)
    row, col = np.divmod(np.arange(PIXELS), COLS)
    target = jnp.concatenate([jnp.asarray(np.stack([row, col], 1), jnp.float32), norm[:, None]], axis=1)
    places = halo_places()
    source_row = np.concatenate([row, np.full(96, 1000), places[0]])
    source_col = np.concatenate([col, np.full(96, 1000), places[1]])
    source = jnp.asarray(np.stack([source_row, source_col]), jnp.float32)
    half = jax.ShapeDtypeStruct((DATE_ROWS, IFGS), jnp.bfloat16)
    weight = jax.ShapeDtypeStruct((PIXELS, DATE_LANES + HALO), jnp.bfloat16)
    whole = pl.BlockSpec(memory_space=pltpu.VMEM)
    return pl.pallas_call(
        operators_kernel,
        in_specs=[whole] * 4,
        out_specs=[whole] * 6,
        out_shape=[half] * 4 + [weight] * 2,
        scratch_shapes=[
            pltpu.VMEM((DATE_LANES, DATE_LANES), jnp.float32),
            pltpu.VMEM((DATE_LANES, 128), jnp.float32),
            pltpu.VMEM((DATE_ROWS, DATE_LANES), jnp.float32),
            pltpu.VMEM((DATE_ROWS, DATE_LANES), jnp.float32),
        ],
        compiler_params=pltpu.CompilerParams(vmem_limit_bytes=32 * MIB),
        cost_estimate=pl.CostEstimate(flops=20_000_000_000, bytes_accessed=5_000_000, transcendentals=0),
        name="operators",
    )(pairs, ordered, target, source)


def project(high_ref, low_ref, data_ref):
    tail = data_ref[:, 2 * OWN_IFGS :, :].reshape(GROUP * IFG_COUNT, 128)
    main, rest = None, None
    for group in range(GROUPS):
        first = data_ref[:, GROUP * group : GROUP * (group + 1), :].reshape(GROUP * IFG_COUNT, 128)
        start = OWN_IFGS + GROUP * group
        second = data_ref[:, start : start + GROUP, :].reshape(GROUP * IFG_COUNT, 128)
        data = split(jnp.concatenate([first, second, tail], axis=1))
        at = slice(512 * group, 512 * group + 512)
        part = dot_split(high_ref[:, at], low_ref[:, at], *data)
        moved = shifted(part[:, 256:], (128 - TAIL * group) % 128)
        main = part[:, :256] if main is None else main + part[:, :256]
        rest = moved if rest is None else rest + moved
    whole = jnp.concatenate([main, rest], axis=1)
    whole = jnp.concatenate([whole, jnp.zeros((DATE_LANES - DATE_ROWS, 384), jnp.float32)], axis=0)
    return whole.T


STEPS = ((0, 1), (0, -1), (1, 0), (-1, 0), (1, 1), (-1, 1), (1, -1), (-1, -1))


def reach(step, length):
    return {1: (length - RIM_WIDTH, length), -1: (0, RIM_WIDTH), 0: (0, length)}[step]


def halo_shape(step):
    (first_col, last_col), (first_row, last_row) = reach(step[0], COLS), reach(step[1], ROWS)
    return range(first_row, last_row), range(first_col, last_col)


def halo_places():
    places = []
    for step in STEPS:
        rows, cols = halo_shape(step)
        places += [(r - ROWS * step[1], c - COLS * step[0]) for r in rows for c in cols]
    places += [(1000, 1000)] * (HALO - len(places))
    return np.array(places).T


def varying_kernel(high_ref, low_ref, data_ref, own_ref, *halo_refs):
    varying = project(high_ref, low_ref, data_ref)
    own_ref[...] = varying[:PIXELS]
    for step, halo_ref in zip(STEPS, halo_refs):
        rows, cols = halo_shape(step)
        for place, row in enumerate(rows):
            first = COLS * row + cols.start
            halo_ref[len(cols) * place : len(cols) * (place + 1), :] = varying[first : first + len(cols)]


def project_varying(high, low, data):
    whole = pl.BlockSpec(memory_space=pltpu.VMEM)
    shapes = [jax.ShapeDtypeStruct((PIXELS, DATE_LANES), jnp.float32)]
    for step in STEPS:
        rows, cols = halo_shape(step)
        shapes.append(jax.ShapeDtypeStruct((len(rows) * len(cols), DATE_LANES), jnp.float32))
    return pl.pallas_call(
        varying_kernel,
        in_specs=[whole] * 3,
        out_specs=[whole] * len(shapes),
        out_shape=shapes,
        compiler_params=pltpu.CompilerParams(vmem_limit_bytes=24 * MIB),
        cost_estimate=pl.CostEstimate(flops=1_100_000_000, bytes_accessed=5_000_000, transcendentals=0),
        name="varying",
    )(high, low, data)


def series_kernel(high_ref, low_ref, data_ref, varying_ref, filter_high, filter_low, series_ref, partial_ref):
    series = project(high_ref, low_ref, data_ref)[:PIXELS]
    for row in range(ROWS):
        series_ref[row] = series[COLS * row : COLS * (row + 1), :DATES]
    own = slice(0, PIXELS)
    smooth = dot_split(filter_high[:, own], filter_low[:, own], *split(varying_ref[...]))
    partial_ref[...] = series - smooth


def project_series(high, low, data, varying, filter_high, filter_low):
    whole = pl.BlockSpec(memory_space=pltpu.VMEM)
    return pl.pallas_call(
        series_kernel,
        in_specs=[whole] * 6,
        out_specs=[whole] * 2,
        out_shape=[
            jax.ShapeDtypeStruct((ROWS, COLS, DATES), jnp.float32),
            jax.ShapeDtypeStruct((PIXELS, DATE_LANES), jnp.float32),
        ],
        compiler_params=pltpu.CompilerParams(vmem_limit_bytes=24 * MIB),
        cost_estimate=pl.CostEstimate(flops=2_000_000_000, bytes_accessed=5_000_000, transcendentals=0),
        name="series",
    )(high, low, data, varying, filter_high, filter_low)


def corrected_kernel(partial_ref, filter_high, filter_low, *refs):
    halo_refs, out_ref = refs[:-1], refs[-1]
    halo = jnp.concatenate([ref[...] for ref in halo_refs], axis=0)
    halo = jnp.concatenate([halo, jnp.zeros((HALO - halo.shape[0], DATE_LANES), jnp.float32)], axis=0)
    at = slice(DATE_LANES, DATE_LANES + HALO)
    result = partial_ref[...] - dot_split(filter_high[:, at], filter_low[:, at], *split(halo))
    for row in range(ROWS):
        out_ref[row] = result[COLS * row : COLS * (row + 1), :DATES]


def correct(partial, filter_high, filter_low, halos):
    whole = pl.BlockSpec(memory_space=pltpu.VMEM)
    return pl.pallas_call(
        corrected_kernel,
        in_specs=[whole] * (3 + len(halos)),
        out_specs=whole,
        out_shape=jax.ShapeDtypeStruct((ROWS, COLS, DATES), jnp.float32),
        compiler_params=pltpu.CompilerParams(vmem_limit_bytes=16 * MIB),
        cost_estimate=pl.CostEstimate(flops=500_000_000, bytes_accessed=3_000_000, transcendentals=0),
        name="corrected",
    )(partial, filter_high, filter_low, *halos)


def passed(value, step):
    pairs = []
    for i in range(IFG_COUNT):
        for b in range(BAND_COUNT):
            to_i, to_b = i + step[0], b + step[1]
            if 0 <= to_i < IFG_COUNT and 0 <= to_b < BAND_COUNT:
                pairs.append((i * BAND_COUNT + b, to_i * BAND_COUNT + to_b))
    return lax.ppermute(value, ("ifg", "band"), pairs)


def edge_weights(start, count, total):
    offsets = jnp.arange(-RIM_WIDTH, RIM_WIDTH + 1, dtype=jnp.int32)
    places = start + jnp.arange(count, dtype=jnp.int32)[:, None] + offsets[None, :]
    inside = ((places >= 0) & (places < total)).astype(jnp.float32)
    return jnp.sum(inside * tap(offsets.astype(jnp.float32))[None, :], axis=1)


def body(unwrapped, component_mask, date_pairs):
    blocks = pack(unwrapped.transpose(1, 0, 2), component_mask.transpose(1, 0, 2))
    data = lax.all_to_all(blocks, "ifg", split_axis=0, concat_axis=0, tiled=True)
    row_norm = edge_weights(lax.axis_index("band") * ROWS, ROWS, ROWS * BAND_COUNT)
    column_norm = edge_weights(lax.axis_index("ifg") * COLS, COLS, COLS * IFG_COUNT)
    norm = (row_norm[:, None] * column_norm[None, :]).reshape(PIXELS)
    inv_high, inv_low, high_high, high_low, filter_high, filter_low = operators(date_pairs, norm)
    varying, *edges = project_varying(high_high, high_low, data)
    halos = [passed(edge, step) for edge, step in zip(edges, STEPS)]
    series, partial = project_series(inv_high, inv_low, data, varying, filter_high, filter_low)
    corrected = correct(partial, filter_high, filter_low, halos)
    return series.transpose(2, 0, 1), corrected.transpose(2, 0, 1)


def solution(mesh):
    placed = (P("ifg", "band", None), P("ifg", "band", None), P())
    return jax.shard_map(
        body,
        mesh=mesh,
        in_specs=placed,
        out_specs=(P(None, "band", "ifg"), P(None, "band", "ifg")),
        check_vma=False,
    )
```

```python
import jax
import jax.numpy as jnp
import numpy as np
from jax import lax
from jax.experimental import pallas as pl
from jax.experimental.pallas import tpu as pltpu
from jax.sharding import PartitionSpec as P

DATES = 300
SPAN = 40
TIME_SIGMA = 6
RIM_WIDTH = 4

DATE_ROWS = 304
DATE_LANES = 384

IFG_COUNT = 32
BAND_COUNT = 16
OWN_IFGS = 48
ROWS = 6
COLS = 48
PIXELS = ROWS * COLS
IFGS = IFG_COUNT * OWN_IFGS

WIDE = COLS + 2 * RIM_WIDTH
WIDE_PIXELS = ROWS * WIDE
LANES = 384

GROUP = 16
GROUPS = OWN_IFGS // GROUP
TAIL = WIDE_PIXELS - 256
SPARE = 128 - TAIL
BLOCK = 2 * OWN_IFGS + 2 * GROUP
SEND_GROUP = 8
SEND_COLS = SEND_GROUP * COLS
SEND_TILES = SEND_COLS // 128

EDGE_PIXELS = RIM_WIDTH * COLS
EDGE_ROWS = 2 * EDGE_PIXELS + EDGE_PIXELS // 2
MIB = 1024 * 1024
WHOLE = pl.BlockSpec(memory_space=pltpu.VMEM)


def split(value):
    high = value.astype(jnp.bfloat16)
    low = (value - high.astype(jnp.float32)).astype(jnp.bfloat16)
    return high, low


def dot(a, b):
    return jnp.dot(a, b, preferred_element_type=jnp.float32)


def full_dot(a, b):
    return jnp.dot(a, b, precision=lax.Precision.HIGHEST, preferred_element_type=jnp.float32)


def pieces(source, target, length):
    while length > 0:
        step = min(length, 128 - source % 128, 128 - target % 128)
        yield source // 128, target // 128, (target - source) % 128, target % 128, target % 128 + step
        source, target, length = source + step, target + step, length - step


def shifted(value, shift):
    return value if shift == 0 else pltpu.roll(value, shift, 1)


def tail_runs(group, source, pixel, length):
    for first, last, base in ((0, TAIL, 128 * group),) if group < 2 else ((0, SPARE, TAIL), (SPARE, TAIL, 128 + TAIL)):
        start, stop = max(pixel, first), min(pixel + length, last)
        if start < stop:
            yield source + start - pixel, base + start - first, stop - start


def pack_kernel(*refs):
    (before, inner, after), out_ref = zip(refs[0:3], refs[3:6]), refs[6]
    step = pl.program_id(0)
    lane = lax.broadcasted_iota(jnp.int32, (OWN_IFGS, 128), 1)
    tail_lane = lax.broadcasted_iota(jnp.int32, (GROUP, 128), 1)

    def masked(pair, row, tile):
        at = (row, slice(None), slice(128 * tile, 128 * tile + 128))
        return pair[0][at] * pair[1][at].astype(jnp.float32)

    tiles = {}
    for row in range(ROWS):
        tiles[row, -1] = jnp.where(step > 0, masked(before, row, 0), 0.0)
        for tile in range(SEND_TILES):
            tiles[row, tile] = masked(inner, row, tile)
        tiles[row, SEND_TILES] = jnp.where(step < pl.num_programs(0) - 1, masked(after, row, 0), 0.0)
    for dest in range(SEND_GROUP):
        out = [jnp.zeros((OWN_IFGS, 128), jnp.float32) for _ in range(2)]
        tail = [jnp.zeros((GROUP, 128), jnp.float32) for _ in range(2)]
        for row in range(ROWS):
            source, target = dest * COLS - RIM_WIDTH, row * WIDE
            length = min(max(256 - target, 0), WIDE)
            for source_tile, tile, shift, first, last in pieces(source, target, length):
                moved = shifted(tiles[row, source_tile], shift)
                out[tile] = jnp.where((lane >= first) & (lane < last), moved, out[tile])
            for group in range(GROUPS):
                for run in tail_runs(group, source + length, target + length - 256, WIDE - length):
                    for source_tile, tile, shift, first, last in pieces(*run):
                        moved = shifted(tiles[row, source_tile][GROUP * group : GROUP * (group + 1)], shift)
                        tail[tile] = jnp.where((tail_lane >= first) & (tail_lane < last), moved, tail[tile])
        out_ref[dest, 0:OWN_IFGS, :] = out[0]
        out_ref[dest, OWN_IFGS : 2 * OWN_IFGS, :] = out[1]
        out_ref[dest, 2 * OWN_IFGS : 2 * OWN_IFGS + GROUP, :] = tail[0]
        out_ref[dest, 2 * OWN_IFGS + GROUP :, :] = tail[1]


def pack(unwrapped, component_mask):
    steps = IFG_COUNT // SEND_GROUP
    last = SEND_TILES * steps - 1
    tile = (ROWS, OWN_IFGS, 128)
    blocks = [
        pl.BlockSpec(tile, lambda i: (0, 0, jnp.maximum(SEND_TILES * i - 1, 0))),
        pl.BlockSpec((ROWS, OWN_IFGS, SEND_COLS), lambda i: (0, 0, i)),
        pl.BlockSpec(tile, lambda i: (0, 0, jnp.minimum(SEND_TILES * (i + 1), last))),
    ]
    return pl.pallas_call(
        pack_kernel,
        grid=(steps,),
        in_specs=blocks + blocks,
        out_specs=pl.BlockSpec((SEND_GROUP, BLOCK, 128), lambda i: (i, 0, 0)),
        out_shape=jax.ShapeDtypeStruct((IFG_COUNT, BLOCK, 128), jnp.float32),
        compiler_params=pltpu.CompilerParams(vmem_limit_bytes=56 * MIB),
        cost_estimate=pl.CostEstimate(flops=2_000_000, bytes_accessed=5_600_000, transcendentals=0),
        name="mask_pack",
    )(*[unwrapped] * 3, *[component_mask] * 3)


def iota(shape, dim):
    return lax.broadcasted_iota(jnp.int32, shape, dim)


def one_hot(pairs, dates):
    date = iota((dates, pairs.shape[1]), 0)
    later = jnp.where(pairs[1:2, :] == date, 1.0, 0.0)
    return (later - jnp.where(pairs[0:1, :] == date, 1.0, 0.0)).astype(jnp.bfloat16)


def identity(rows, cols, first=0):
    return jnp.where(iota((rows, cols), 0) + first == iota((rows, cols), 1), 1.0, 0.0)


def eliminate(normal_ref, band_ref, lower_ref, scaled_ref):
    window = SPAN // 8 + 1
    blocks = DATE_ROWS // 8
    for tile in range(window, window + blocks):
        start = 8 * tile - SPAN
        rows = normal_ref[8 * tile : 8 * tile + 8, :]
        band_ref[8 * tile : 8 * tile + 8, :] = pltpu.roll(rows, (DATE_LANES - start) % DATE_LANES, 1)[:, :128]
    sub = iota((8, 128), 0)
    lane = iota((8, 128), 1)

    def block_step(block, carry):
        left, right = list(carry[:window]), list(carry[window:])
        pivots = jnp.zeros((8, 128), jnp.float32)
        for j in range(8):
            pivot_row = left[0][j : j + 1, :]
            right_row = right[0][j : j + 1, :]
            scale = jnp.broadcast_to(1.0 / pivot_row[:, j : j + 1], (8, 128))
            pivots = jnp.where(sub == j, scale, pivots)
            scaled_row = pivot_row * scale[0:1, :]
            scaled_right = right_row * jnp.concatenate([scale[0:1, :]] * 3, axis=1)
            for q in range(window):
                factor = jnp.broadcast_to(left[q][:, j : j + 1], (8, 128))
                if q == 0:
                    factor = jnp.where(sub > j, factor, 0.0)
                left[q] = left[q] - factor * scaled_row
                right[q] = right[q] - jnp.concatenate([factor] * 3, axis=1) * scaled_right
        at = pl.ds(pl.multiple_of(8 * block, 8), 8)
        lower_ref[at, :] = right[0]
        scaled_ref[at, :] = right[0] * jnp.concatenate([pivots] * 3, axis=1)
        entering = pl.multiple_of(8 * (block + window), 8)
        left = [jnp.where(lane < 120, pltpu.roll(part, 120, 1), 0.0) for part in left[1:]]
        left.append(band_ref[pl.ds(entering, 8), :])
        right = right[1:] + [identity(8, DATE_LANES, entering)]
        return tuple(left + right)

    left = [normal_ref[8 * q : 8 * q + 8, 0:128] for q in range(window)]
    right = [identity(8, DATE_LANES, 8 * q) for q in range(window)]
    lax.fori_loop(0, blocks, block_step, tuple(left + right))


def highpass_matrix():
    row, col = iota((DATE_ROWS, DATE_LANES), 0), iota((DATE_ROWS, DATE_LANES), 1)
    spread = (row - col).astype(jnp.float32)
    weights = jnp.exp(-spread * spread / (2.0 * TIME_SIGMA * TIME_SIGMA))
    weights = jnp.where(col < DATES, weights, 0.0)
    lowpass = weights / jnp.sum(weights, axis=1, keepdims=True)
    return jnp.where((row < DATES) & (col < DATES), identity(DATE_ROWS, DATE_LANES) - lowpass, 0.0)


def tap(offset):
    sigma = RIM_WIDTH / 2.0
    return jnp.where(jnp.abs(offset) <= RIM_WIDTH, jnp.exp(-offset * offset / (2.0 * sigma * sigma)), 0.0)


def operators_kernel(pairs_ref, target_ref, source_ref, solve_ref, filtered_ref, filter_high, filter_low,
                     normal_ref, band_ref, lower_ref, scaled_ref):
    design = one_hot(pairs_ref[...], DATE_LANES)
    normal = lax.dot_general(design, design, (((1,), (1,)), ((), ())), preferred_element_type=jnp.float32)
    normal_ref[...] = normal + identity(DATE_LANES, DATE_LANES)
    eliminate(normal_ref, band_ref, lower_ref, scaled_ref)
    solve = lax.dot_general(lower_ref[...], scaled_ref[...], (((0,), (0,)), ((), ())),
                            precision=lax.Precision.HIGHEST, preferred_element_type=jnp.float32)
    solve_ref[...] = solve[:DATE_ROWS]
    filtered_ref[...] = full_dot(highpass_matrix(), solve)
    same_row = source_ref[:, 0:1] == target_ref[0:1, :]
    weights = tap(source_ref[:, 1:2] - target_ref[1:2, :]) / target_ref[2:3, :]
    filter_high[...], filter_low[...] = split(jnp.where(same_row, weights, 0.0))


def operators(pairs, column_norm):
    row, col = np.divmod(np.arange(PIXELS), COLS)
    place = np.stack([np.append(row, np.full(LANES - PIXELS, 2000)), np.append(col, np.zeros(LANES - PIXELS))])
    norm = jnp.concatenate([jnp.tile(column_norm, ROWS), jnp.ones(LANES - PIXELS, jnp.float32)])
    target = jnp.concatenate([jnp.asarray(place, jnp.float32), norm[None, :]], axis=0)
    row, col = np.divmod(np.arange(LANES), WIDE)
    source = jnp.asarray(np.stack([row, col - RIM_WIDTH], 1), jnp.float32)
    square = jax.ShapeDtypeStruct((DATE_ROWS, DATE_LANES), jnp.float32)
    weight = jax.ShapeDtypeStruct((LANES, LANES), jnp.bfloat16)
    return pl.pallas_call(
        operators_kernel,
        in_specs=[WHOLE] * 3,
        out_specs=[WHOLE] * 4,
        out_shape=[square] * 2 + [weight] * 2,
        scratch_shapes=[
            pltpu.VMEM((DATE_LANES, DATE_LANES), jnp.float32),
            pltpu.VMEM((DATE_LANES, 128), jnp.float32),
            pltpu.VMEM((DATE_ROWS, DATE_LANES), jnp.float32),
            pltpu.VMEM((DATE_ROWS, DATE_LANES), jnp.float32),
        ],
        compiler_params=pltpu.CompilerParams(vmem_limit_bytes=24 * MIB),
        cost_estimate=pl.CostEstimate(flops=20_000_000_000, bytes_accessed=3_000_000, transcendentals=0),
        name="operators",
    )(pairs, target, source)


def padded(value):
    return jnp.concatenate([value, jnp.zeros((DATE_LANES - DATE_ROWS, LANES), jnp.float32)], axis=0)


def gather_dates(ordered_ref, data_ref):
    def block(start):
        return split(data_ref[:, start : start + GROUP, :].reshape(GROUP * IFG_COUNT, 128))

    tails = [block(2 * OWN_IFGS), block(2 * OWN_IFGS + GROUP)]
    main, rest, spare = None, None, None
    for group in range(GROUPS):
        parts = [block(GROUP * group), block(OWN_IFGS + GROUP * group)]
        parts += tails if group == 2 else [tails[group]]
        design = one_hot(ordered_ref[:, 512 * group : 512 * group + 512], DATE_ROWS)
        high = jnp.concatenate([part[0] for part in parts], axis=1)
        low = jnp.concatenate([part[1] for part in parts], axis=1)
        sums = dot(design, high) + dot(design, low)
        main = sums[:, :256] if main is None else main + sums[:, :256]
        if group == 2:
            spare = sums[:, 256:]
        else:
            rest = sums[:, 256:] if rest is None else rest + sums[:, 256:]
    lane = iota((DATE_ROWS, 128), 1)
    first, second = shifted(spare[:, :128], 128 - TAIL), shifted(spare[:, 128:], 128 - TAIL + SPARE)
    rest = jnp.where(lane < TAIL, rest + jnp.where(lane < SPARE, first, second), 0.0)
    return jnp.concatenate([main, rest], axis=1)


def varying_kernel(ordered_ref, data_ref, filtered_ref, filter_high, filter_low, sums_ref, own_ref, top_ref, bottom_ref):
    sums = padded(gather_dates(ordered_ref, data_ref))
    sums_ref[...] = sums
    high, low = split(full_dot(filtered_ref[...], sums))
    smooth = dot(high, filter_high[...]) + (dot(high, filter_low[...]) + dot(low, filter_high[...]))
    smooth = padded(smooth).T
    own_ref[...] = smooth[:PIXELS]
    lane = iota((EDGE_PIXELS // 2, 128), 1)
    for edge_ref, first in ((top_ref, 0), (bottom_ref, PIXELS - EDGE_PIXELS)):
        edge = smooth[first : first + EDGE_PIXELS]
        edge_ref[0:EDGE_PIXELS, :] = edge[:, 0:128]
        edge_ref[EDGE_PIXELS : 2 * EDGE_PIXELS, :] = edge[:, 128:256]
        rest = edge[:, 256:]
        moved = pltpu.roll(rest[EDGE_PIXELS // 2 :], 64, 1)
        edge_ref[2 * EDGE_PIXELS :, :] = jnp.where(lane < 64, rest[: EDGE_PIXELS // 2], moved)


def project_varying(ordered, data, filtered, filter_high, filter_low):
    edge = jax.ShapeDtypeStruct((EDGE_ROWS, 128), jnp.float32)
    return pl.pallas_call(
        varying_kernel,
        in_specs=[WHOLE] * 5,
        out_specs=[WHOLE] * 4,
        out_shape=[
            jax.ShapeDtypeStruct((DATE_LANES, LANES), jnp.float32),
            jax.ShapeDtypeStruct((PIXELS, DATE_LANES), jnp.float32),
            edge,
            edge,
        ],
        compiler_params=pltpu.CompilerParams(vmem_limit_bytes=24 * MIB),
        cost_estimate=pl.CostEstimate(flops=1_100_000_000, bytes_accessed=5_000_000, transcendentals=0),
        name="varying",
    )(ordered, data, filtered, filter_high, filter_low)


def weight(offset):
    sigma = RIM_WIDTH / 2.0
    return float(np.exp(-offset * offset / (2.0 * sigma * sigma)))


def series_kernel(scale_ref, solve_ref, sums_ref, smooth_ref, series_ref, partial_ref):
    series = padded(full_dot(solve_ref[...], sums_ref[...])).T
    for row in range(ROWS):
        start = WIDE * row + RIM_WIDTH
        own = series[start : start + COLS]
        series_ref[row] = own[:, :DATES]
        total = None
        for other in range(ROWS):
            if abs(other - row) <= RIM_WIDTH:
                term = weight(other - row) * smooth_ref[COLS * other : COLS * (other + 1), :]
                total = term if total is None else total + term
        partial_ref[COLS * row : COLS * (row + 1), :] = own - total * scale_ref[row]


def project_series(row_scale, solve, sums, smooth):
    return pl.pallas_call(
        series_kernel,
        in_specs=[pl.BlockSpec(memory_space=pltpu.SMEM)] + [WHOLE] * 3,
        out_specs=[WHOLE] * 2,
        out_shape=[
            jax.ShapeDtypeStruct((ROWS, COLS, DATES), jnp.float32),
            jax.ShapeDtypeStruct((PIXELS, DATE_LANES), jnp.float32),
        ],
        compiler_params=pltpu.CompilerParams(vmem_limit_bytes=16 * MIB),
        cost_estimate=pl.CostEstimate(flops=2_000_000_000, bytes_accessed=2_000_000, transcendentals=0),
        name="series",
    )(row_scale, solve, sums, smooth)


def edge_tile(edge_ref, row, tile):
    if tile < 2:
        start = EDGE_PIXELS * tile + COLS * row
        return edge_ref[start : start + COLS, :]
    start = 2 * EDGE_PIXELS + COLS * (row % 2)
    return shifted(edge_ref[start : start + COLS, :], 64 * (row // 2))


def corrected_kernel(scale_ref, partial_ref, above_ref, below_ref, out_ref):
    for tile in range(3):
        above = [edge_tile(above_ref, row, tile) for row in range(RIM_WIDTH)]
        below = [edge_tile(below_ref, row, tile) for row in range(RIM_WIDTH)]
        for row in range(ROWS):
            near = [(other - RIM_WIDTH - row, above[other]) for other in range(RIM_WIDTH)]
            near += [(ROWS + other - row, below[other]) for other in range(RIM_WIDTH)]
            total = sum(weight(offset) * value for offset, value in near if abs(offset) <= RIM_WIDTH)
            part = partial_ref[COLS * row : COLS * (row + 1), 128 * tile : 128 * (tile + 1)]
            width = min(128, DATES - 128 * tile)
            out_ref[row, :, 128 * tile : 128 * tile + width] = (part - total * scale_ref[row])[:, :width]


def correct(row_scale, partial, above, below):
    return pl.pallas_call(
        corrected_kernel,
        in_specs=[pl.BlockSpec(memory_space=pltpu.SMEM)] + [WHOLE] * 3,
        out_specs=WHOLE,
        out_shape=jax.ShapeDtypeStruct((ROWS, COLS, DATES), jnp.float32),
        compiler_params=pltpu.CompilerParams(vmem_limit_bytes=16 * MIB),
        cost_estimate=pl.CostEstimate(flops=1_000_000, bytes_accessed=1_400_000, transcendentals=0),
        name="corrected",
    )(row_scale, partial, above, below)


def edge_weights(start, count, total):
    offsets = jnp.arange(-RIM_WIDTH, RIM_WIDTH + 1, dtype=jnp.int32)
    places = start + jnp.arange(count, dtype=jnp.int32)[:, None] + offsets[None, :]
    inside = ((places >= 0) & (places < total)).astype(jnp.float32)
    return jnp.sum(inside * tap(offsets.astype(jnp.float32))[None, :], axis=1)


def body(unwrapped, component_mask, date_pairs):
    blocks = pack(unwrapped.transpose(1, 0, 2), component_mask.transpose(1, 0, 2))
    data = lax.all_to_all(blocks, "ifg", split_axis=0, concat_axis=0, tiled=True)
    row_scale = 1.0 / edge_weights(lax.axis_index("band") * ROWS, ROWS, ROWS * BAND_COUNT)
    column_norm = edge_weights(lax.axis_index("ifg") * COLS, COLS, COLS * IFG_COUNT)
    pairs = date_pairs.T
    ordered = pairs.reshape(2, IFG_COUNT, GROUPS, GROUP).transpose(0, 2, 1, 3).reshape(2, IFGS)
    solve, filtered, filter_high, filter_low = operators(pairs, column_norm)
    sums, smooth, top, bottom = project_varying(ordered, data, filtered, filter_high, filter_low)
    down = [(i, i + 1) for i in range(BAND_COUNT - 1)]
    above = lax.ppermute(bottom, "band", down)
    below = lax.ppermute(top, "band", [(j, i) for i, j in down])
    series, partial = project_series(row_scale, solve, sums, smooth)
    corrected = correct(row_scale, partial, above, below)
    return series.transpose(2, 0, 1), corrected.transpose(2, 0, 1)


def solution(mesh):
    placed = (P("ifg", "band", None), P("ifg", "band", None), P())
    return jax.shard_map(
        body,
        mesh=mesh,
        in_specs=placed,
        out_specs=(P(None, "band", "ifg"), P(None, "band", "ifg")),
        check_vma=False,
    )
```

```python
import jax
import jax.numpy as jnp
import numpy as np
from jax import lax
from jax.experimental import pallas as pl
from jax.experimental.pallas import tpu as pltpu
from jax.sharding import PartitionSpec as P

DATES = 300
SPAN = 40
TIME_SIGMA = 6
RIM_WIDTH = 4

DATE_ROWS = 304
DATE_LANES = 384

IFG_COUNT = 32
BAND_COUNT = 16
OWN_IFGS = 48
ROWS = 6
COLS = 48
PIXELS = ROWS * COLS
IFGS = IFG_COUNT * OWN_IFGS

WIDE = COLS + 2 * RIM_WIDTH
WIDE_PIXELS = ROWS * WIDE
LANES = 384

GROUP = 16
GROUPS = OWN_IFGS // GROUP
TAIL = WIDE_PIXELS - 256
SPARE = 128 - TAIL
BLOCK = 2 * OWN_IFGS + 2 * GROUP
CHUNKS = 4
CHUNK = IFG_COUNT * COLS // CHUNKS
STORE = 4

EDGE_PIXELS = RIM_WIDTH * COLS
EDGE_ROWS = 2 * EDGE_PIXELS + EDGE_PIXELS // 2
MIB = 1024 * 1024
WHOLE = pl.BlockSpec(memory_space=pltpu.VMEM)


def split(value):
    high = value.astype(jnp.bfloat16)
    low = (value - high.astype(jnp.float32)).astype(jnp.bfloat16)
    return high, low


def dot(a, b):
    return jnp.dot(a, b, preferred_element_type=jnp.float32)


def full_dot(a, b):
    return jnp.dot(a, b, precision=lax.Precision.HIGHEST, preferred_element_type=jnp.float32)


def pieces(source, target, length):
    while length > 0:
        step = min(length, 128 - source % 128, 128 - target % 128)
        yield source // 128, target // 128, (target - source) % 128, target % 128, target % 128 + step
        source, target, length = source + step, target + step, length - step


def shifted(value, shift):
    return value if shift == 0 else pltpu.roll(value, shift, 1)


def tail_runs(group, source, pixel, length):
    for first, last, base in ((0, TAIL, 128 * group),) if group < 2 else ((0, SPARE, TAIL), (SPARE, TAIL, 128 + TAIL)):
        start, stop = max(pixel, first), min(pixel + length, last)
        if start < stop:
            yield source + start - pixel, base + start - first, stop - start


def needed_chunk(dest):
    last = dest * COLS + COLS + RIM_WIDTH - 1
    return min(last, IFG_COUNT * COLS - 1) // CHUNK


def pack_kernel(unwrapped_ref, mask_ref, out_ref, phase, mask, masked, block, in_sem, out_sem):
    loads = []
    for chunk in range(CHUNKS):
        at = (slice(None), slice(None), pl.ds(CHUNK * chunk, CHUNK))
        pair = (
            pltpu.make_async_copy(unwrapped_ref.at[at], phase.at[at], in_sem.at[0, chunk]),
            pltpu.make_async_copy(mask_ref.at[at], mask.at[at], in_sem.at[1, chunk]),
        )
        for load in pair:
            load.start()
        loads.append(pair)
    width = CHUNKS * CHUNK
    for row in range(ROWS):
        masked[row, :, 0:128] = jnp.zeros((OWN_IFGS, 128), jnp.float32)
        masked[row, :, 128 + width : 256 + width] = jnp.zeros((OWN_IFGS, 128), jnp.float32)
    lane = lax.broadcasted_iota(jnp.int32, (GROUP, 128), 1)

    def place(parts, rows, row, source, target, length):
        for source_tile, tile, shift, first, last in pieces(source, target, length):
            moved = shifted(masked[row, rows, 128 * source_tile : 128 * source_tile + 128], shift)
            parts[tile] = jnp.where((lane >= first) & (lane < last), moved, parts[tile])

    def fill(dest):
        tail = [jnp.zeros((GROUP, 128), jnp.float32)] * 2
        for group in range(GROUPS):
            rows = slice(GROUP * group, GROUP * (group + 1))
            main = [jnp.zeros((GROUP, 128), jnp.float32)] * 2
            for row in range(ROWS):
                source, target = 128 + dest * COLS - RIM_WIDTH, row * WIDE
                length = min(max(256 - target, 0), WIDE)
                place(main, rows, row, source, target, length)
                for run in tail_runs(group, source + length, target + length - 256, WIDE - length):
                    place(tail, rows, row, *run)
            block[dest, rows, :] = main[0]
            block[dest, OWN_IFGS + GROUP * group : OWN_IFGS + GROUP * (group + 1), :] = main[1]
        block[dest, 2 * OWN_IFGS : 2 * OWN_IFGS + GROUP, :] = tail[0]
        block[dest, 2 * OWN_IFGS + GROUP :, :] = tail[1]

    stores = []
    for chunk in range(CHUNKS):
        for load in loads[chunk]:
            load.wait()
        for row in range(ROWS):
            first = CHUNK * chunk
            values = phase[row, :, first : first + CHUNK] * mask[row, :, first : first + CHUNK].astype(jnp.float32)
            masked[row, :, 128 + first : 128 + first + CHUNK] = values
        for dest in range(IFG_COUNT):
            if needed_chunk(dest) == chunk:
                fill(dest)
                if (dest + 1) % STORE == 0:
                    at = pl.ds(dest + 1 - STORE, STORE)
                    store = pltpu.make_async_copy(block.at[at], out_ref.at[at], out_sem.at[dest // STORE])
                    store.start()
                    stores.append(store)
    for store in stores:
        store.wait()


def pack(unwrapped, component_mask):
    anywhere = pl.BlockSpec(memory_space=pl.ANY)
    columns = CHUNKS * CHUNK
    return pl.pallas_call(
        pack_kernel,
        in_specs=[anywhere] * 2,
        out_specs=anywhere,
        out_shape=jax.ShapeDtypeStruct((IFG_COUNT, BLOCK, 128), jnp.float32),
        scratch_shapes=[
            pltpu.VMEM((ROWS, OWN_IFGS, columns), jnp.float32),
            pltpu.VMEM((ROWS, OWN_IFGS, columns), jnp.int32),
            pltpu.VMEM((ROWS, OWN_IFGS, columns + 256), jnp.float32),
            pltpu.VMEM((IFG_COUNT, BLOCK, 128), jnp.float32),
            pltpu.SemaphoreType.DMA((2, CHUNKS)),
            pltpu.SemaphoreType.DMA((IFG_COUNT // STORE,)),
        ],
        compiler_params=pltpu.CompilerParams(vmem_limit_bytes=56 * MIB),
        cost_estimate=pl.CostEstimate(flops=2_000_000, bytes_accessed=5_600_000, transcendentals=0),
        name="mask_pack",
    )(unwrapped, component_mask)


def iota(shape, dim):
    return lax.broadcasted_iota(jnp.int32, shape, dim)


def one_hot(pairs, dates):
    date = iota((dates, pairs.shape[1]), 0)
    later = jnp.where(pairs[1:2, :] == date, 1.0, 0.0)
    return (later - jnp.where(pairs[0:1, :] == date, 1.0, 0.0)).astype(jnp.bfloat16)


def identity(rows, cols, first=0):
    return jnp.where(iota((rows, cols), 0) + first == iota((rows, cols), 1), 1.0, 0.0)


def eliminate(normal_ref, band_ref, lower_ref, scaled_ref):
    window = SPAN // 8 + 1
    blocks = DATE_ROWS // 8
    for tile in range(window, window + blocks):
        start = 8 * tile - SPAN
        rows = normal_ref[8 * tile : 8 * tile + 8, :]
        band_ref[8 * tile : 8 * tile + 8, :] = pltpu.roll(rows, (DATE_LANES - start) % DATE_LANES, 1)[:, :128]
    sub = iota((8, 128), 0)
    lane = iota((8, 128), 1)

    def block_step(block, carry):
        left, right = list(carry[:window]), list(carry[window:])
        pivots = jnp.zeros((8, 128), jnp.float32)
        for j in range(8):
            pivot_row = left[0][j : j + 1, :]
            right_row = right[0][j : j + 1, :]
            scale = jnp.broadcast_to(1.0 / pivot_row[:, j : j + 1], (8, 128))
            pivots = jnp.where(sub == j, scale, pivots)
            scaled_row = pivot_row * scale[0:1, :]
            scaled_right = right_row * jnp.concatenate([scale[0:1, :]] * 3, axis=1)
            for q in range(window):
                factor = jnp.broadcast_to(left[q][:, j : j + 1], (8, 128))
                if q == 0:
                    factor = jnp.where(sub > j, factor, 0.0)
                left[q] = left[q] - factor * scaled_row
                right[q] = right[q] - jnp.concatenate([factor] * 3, axis=1) * scaled_right
        at = pl.ds(pl.multiple_of(8 * block, 8), 8)
        lower_ref[at, :] = right[0]
        scaled_ref[at, :] = right[0] * jnp.concatenate([pivots] * 3, axis=1)
        entering = pl.multiple_of(8 * (block + window), 8)
        left = [jnp.where(lane < 120, pltpu.roll(part, 120, 1), 0.0) for part in left[1:]]
        left.append(band_ref[pl.ds(entering, 8), :])
        right = right[1:] + [identity(8, DATE_LANES, entering)]
        return tuple(left + right)

    left = [normal_ref[8 * q : 8 * q + 8, 0:128] for q in range(window)]
    right = [identity(8, DATE_LANES, 8 * q) for q in range(window)]
    lax.fori_loop(0, blocks, block_step, tuple(left + right))


def highpass_matrix():
    row, col = iota((DATE_ROWS, DATE_LANES), 0), iota((DATE_ROWS, DATE_LANES), 1)
    spread = (row - col).astype(jnp.float32)
    weights = jnp.exp(-spread * spread / (2.0 * TIME_SIGMA * TIME_SIGMA))
    weights = jnp.where(col < DATES, weights, 0.0)
    lowpass = weights / jnp.sum(weights, axis=1, keepdims=True)
    return jnp.where((row < DATES) & (col < DATES), identity(DATE_ROWS, DATE_LANES) - lowpass, 0.0)


def tap(offset):
    sigma = RIM_WIDTH / 2.0
    return jnp.where(jnp.abs(offset) <= RIM_WIDTH, jnp.exp(-offset * offset / (2.0 * sigma * sigma)), 0.0)


def split_three(value):
    first = value.astype(jnp.bfloat16)
    rest = value - first.astype(jnp.float32)
    second = rest.astype(jnp.bfloat16)
    return first, second, (rest - second.astype(jnp.float32)).astype(jnp.bfloat16)


def operators_kernel(pairs_ref, solve_ref, first_ref, second_ref, third_ref, normal_ref, band_ref, lower_ref, scaled_ref):
    design = one_hot(pairs_ref[...], DATE_LANES)
    normal = lax.dot_general(design, design, (((1,), (1,)), ((), ())), preferred_element_type=jnp.float32)
    normal_ref[...] = normal + identity(DATE_LANES, DATE_LANES)
    eliminate(normal_ref, band_ref, lower_ref, scaled_ref)
    solve = lax.dot_general(lower_ref[...], scaled_ref[...], (((0,), (0,)), ((), ())),
                            precision=lax.Precision.HIGHEST, preferred_element_type=jnp.float32)
    solve_ref[...] = solve[:DATE_ROWS]
    first_ref[...], second_ref[...], third_ref[...] = split_three(full_dot(highpass_matrix(), solve))


def operators(pairs):
    part = jax.ShapeDtypeStruct((DATE_ROWS, DATE_LANES), jnp.bfloat16)
    return pl.pallas_call(
        operators_kernel,
        in_specs=[WHOLE],
        out_specs=[WHOLE] * 4,
        out_shape=[jax.ShapeDtypeStruct((DATE_ROWS, DATE_LANES), jnp.float32)] + [part] * 3,
        scratch_shapes=[
            pltpu.VMEM((DATE_LANES, DATE_LANES), jnp.float32),
            pltpu.VMEM((DATE_LANES, 128), jnp.float32),
            pltpu.VMEM((DATE_ROWS, DATE_LANES), jnp.float32),
            pltpu.VMEM((DATE_ROWS, DATE_LANES), jnp.float32),
        ],
        compiler_params=pltpu.CompilerParams(vmem_limit_bytes=24 * MIB),
        cost_estimate=pl.CostEstimate(flops=20_000_000_000, bytes_accessed=3_000_000, transcendentals=0),
        name="operators",
    )(pairs)


def padded(value):
    return jnp.concatenate([value, jnp.zeros((DATE_LANES - DATE_ROWS, LANES), jnp.float32)], axis=0)


def gather_dates(ordered_ref, data_ref):
    def block(start):
        return split(data_ref[:, start : start + GROUP, :].reshape(GROUP * IFG_COUNT, 128))

    tails = [block(2 * OWN_IFGS), block(2 * OWN_IFGS + GROUP)]
    main, rest, spare = None, None, None
    for group in range(GROUPS):
        parts = [block(GROUP * group), block(OWN_IFGS + GROUP * group)]
        parts += tails if group == 2 else [tails[group]]
        design = one_hot(ordered_ref[:, 512 * group : 512 * group + 512], DATE_ROWS)
        high = jnp.concatenate([part[0] for part in parts], axis=1)
        low = jnp.concatenate([part[1] for part in parts], axis=1)
        sums = dot(design, high) + dot(design, low)
        main = sums[:, :256] if main is None else main + sums[:, :256]
        if group == 2:
            spare = sums[:, 256:]
        else:
            rest = sums[:, 256:] if rest is None else rest + sums[:, 256:]
    lane = iota((DATE_ROWS, 128), 1)
    first, second = shifted(spare[:, :128], 128 - TAIL), shifted(spare[:, 128:], 128 - TAIL + SPARE)
    rest = jnp.where(lane < TAIL, rest + jnp.where(lane < SPARE, first, second), 0.0)
    return jnp.concatenate([main, rest], axis=1)


def weight(offset):
    sigma = RIM_WIDTH / 2.0
    return float(np.exp(-offset * offset / (2.0 * sigma * sigma)))


def varying_kernel(ordered_ref, data_ref, first_ref, second_ref, third_ref, scale_ref, sums_ref, own_ref, top_ref,
                   bottom_ref, wide_ref):
    sums = padded(gather_dates(ordered_ref, data_ref))
    sums_ref[...] = sums
    left = [first_ref[...], second_ref[...], third_ref[...]]
    right = split_three(sums)
    orders = ((2, 0), (0, 2), (1, 1), (1, 0), (0, 1), (0, 0))
    varying = dot(
        jnp.concatenate([left[i] for i, _ in orders], axis=1), jnp.concatenate([right[j] for _, j in orders], axis=0)
    )
    varying = padded(varying).T
    half = RIM_WIDTH // 2
    lane = iota((COLS, 128), 1)
    kept = {}
    for tile in range(3):
        wide_ref[tile] = varying[:, 128 * tile : 128 * (tile + 1)]
        for row in range(ROWS):
            start = WIDE * row + RIM_WIDTH
            total = wide_ref[tile, start : start + COLS, :]
            for offset in range(1, RIM_WIDTH + 1):
                both = wide_ref[tile, start - offset : start - offset + COLS, :]
                both = both + wide_ref[tile, start + offset : start + offset + COLS, :]
                total = total + weight(offset) * both
            total = total * scale_ref[...]
            own_ref[COLS * row : COLS * (row + 1), 128 * tile : 128 * (tile + 1)] = total
            for edge_ref, place in ((top_ref, row), (bottom_ref, row - (ROWS - RIM_WIDTH))):
                if 0 <= place < RIM_WIDTH:
                    if tile < 2:
                        edge_ref[EDGE_PIXELS * tile + COLS * place : EDGE_PIXELS * tile + COLS * (place + 1), :] = total
                    elif place < half:
                        kept[row - place, place] = total
                    else:
                        start_row = 2 * EDGE_PIXELS + COLS * (place - half)
                        packed = jnp.where(lane < 64, kept[row - place, place - half], pltpu.roll(total, 64, 1))
                        edge_ref[start_row : start_row + COLS, :] = packed


def project_varying(ordered, data, filtered, column_scale):
    edge = jax.ShapeDtypeStruct((EDGE_ROWS, 128), jnp.float32)
    return pl.pallas_call(
        varying_kernel,
        in_specs=[WHOLE] * 6,
        out_specs=[WHOLE] * 4,
        out_shape=[
            jax.ShapeDtypeStruct((DATE_LANES, LANES), jnp.float32),
            jax.ShapeDtypeStruct((PIXELS, DATE_LANES), jnp.float32),
            edge,
            edge,
        ],
        scratch_shapes=[pltpu.VMEM((3, LANES, 128), jnp.float32)],
        compiler_params=pltpu.CompilerParams(vmem_limit_bytes=24 * MIB),
        cost_estimate=pl.CostEstimate(flops=1_100_000_000, bytes_accessed=5_000_000, transcendentals=0),
        name="varying",
    )(ordered, data, *filtered, column_scale)


def series_kernel(scale_ref, solve_ref, sums_ref, smooth_ref, series_ref, partial_ref):
    series = padded(full_dot(solve_ref[...], sums_ref[...])).T
    for row in range(ROWS):
        start = WIDE * row + RIM_WIDTH
        own = series[start : start + COLS]
        series_ref[row] = own[:, :DATES]
        total = None
        for other in range(ROWS):
            if abs(other - row) <= RIM_WIDTH:
                term = weight(other - row) * smooth_ref[COLS * other : COLS * (other + 1), :]
                total = term if total is None else total + term
        partial_ref[COLS * row : COLS * (row + 1), :] = own - total * scale_ref[row]


def project_series(row_scale, solve, sums, smooth):
    return pl.pallas_call(
        series_kernel,
        in_specs=[pl.BlockSpec(memory_space=pltpu.SMEM)] + [WHOLE] * 3,
        out_specs=[WHOLE] * 2,
        out_shape=[
            jax.ShapeDtypeStruct((ROWS, COLS, DATES), jnp.float32),
            jax.ShapeDtypeStruct((PIXELS, DATE_LANES), jnp.float32),
        ],
        compiler_params=pltpu.CompilerParams(vmem_limit_bytes=16 * MIB),
        cost_estimate=pl.CostEstimate(flops=2_000_000_000, bytes_accessed=2_000_000, transcendentals=0),
        name="series",
    )(row_scale, solve, sums, smooth)


def edge_tile(edge_ref, row, tile):
    if tile < 2:
        start = EDGE_PIXELS * tile + COLS * row
        return edge_ref[start : start + COLS, :]
    start = 2 * EDGE_PIXELS + COLS * (row % 2)
    return shifted(edge_ref[start : start + COLS, :], 64 * (row // 2))


def corrected_kernel(scale_ref, partial_ref, above_ref, below_ref, out_ref, rows_ref, sem):
    stores = []
    for row in range(ROWS):
        for tile in range(3):
            near = [(other - RIM_WIDTH - row, above_ref, other) for other in range(RIM_WIDTH)]
            near += [(ROWS + other - row, below_ref, other) for other in range(RIM_WIDTH)]
            total = sum(weight(off) * edge_tile(ref, other, tile) for off, ref, other in near if abs(off) <= RIM_WIDTH)
            part = partial_ref[COLS * row : COLS * (row + 1), 128 * tile : 128 * (tile + 1)]
            width = min(128, DATES - 128 * tile)
            rows_ref[row, :, 128 * tile : 128 * tile + width] = (part - total * scale_ref[row])[:, :width]
        store = pltpu.make_async_copy(rows_ref.at[row], out_ref.at[row], sem.at[row])
        store.start()
        stores.append(store)
    for store in stores:
        store.wait()


def correct(row_scale, partial, above, below):
    return pl.pallas_call(
        corrected_kernel,
        in_specs=[pl.BlockSpec(memory_space=pltpu.SMEM)] + [WHOLE] * 3,
        out_specs=pl.BlockSpec(memory_space=pl.ANY),
        out_shape=jax.ShapeDtypeStruct((ROWS, COLS, DATES), jnp.float32),
        scratch_shapes=[pltpu.VMEM((ROWS, COLS, DATES), jnp.float32), pltpu.SemaphoreType.DMA((ROWS,))],
        compiler_params=pltpu.CompilerParams(vmem_limit_bytes=16 * MIB),
        cost_estimate=pl.CostEstimate(flops=1_000_000, bytes_accessed=1_400_000, transcendentals=0),
        name="corrected",
    )(row_scale, partial, above, below)


def edge_weights(start, count, total):
    offsets = jnp.arange(-RIM_WIDTH, RIM_WIDTH + 1, dtype=jnp.int32)
    places = start + jnp.arange(count, dtype=jnp.int32)[:, None] + offsets[None, :]
    inside = ((places >= 0) & (places < total)).astype(jnp.float32)
    return jnp.sum(inside * tap(offsets.astype(jnp.float32))[None, :], axis=1)


def body(unwrapped, component_mask, date_pairs):
    blocks = pack(unwrapped.transpose(1, 0, 2), component_mask.transpose(1, 0, 2))
    data = lax.all_to_all(blocks, "ifg", split_axis=0, concat_axis=0, tiled=True)
    row_scale = 1.0 / edge_weights(lax.axis_index("band") * ROWS, ROWS, ROWS * BAND_COUNT)
    column_norm = edge_weights(lax.axis_index("ifg") * COLS, COLS, COLS * IFG_COUNT)
    pairs = date_pairs.T
    ordered = pairs.reshape(2, IFG_COUNT, GROUPS, GROUP).transpose(0, 2, 1, 3).reshape(2, IFGS)
    column_scale = jnp.broadcast_to((1.0 / column_norm)[:, None], (COLS, 128))
    solve, *filtered = operators(pairs)
    sums, smooth, top, bottom = project_varying(ordered, data, filtered, column_scale)
    down = [(i, i + 1) for i in range(BAND_COUNT - 1)]
    above = lax.ppermute(bottom, "band", down)
    below = lax.ppermute(top, "band", [(j, i) for i, j in down])
    series, partial = project_series(row_scale, solve, sums, smooth)
    corrected = correct(row_scale, partial, above, below)
    return series.transpose(2, 0, 1), corrected.transpose(2, 0, 1)


def solution(mesh):
    placed = (P("ifg", "band", None), P("ifg", "band", None), P())
    return jax.shard_map(
        body,
        mesh=mesh,
        in_specs=placed,
        out_specs=(P(None, "band", "ifg"), P(None, "band", "ifg")),
        check_vma=False,
    )
```

```python
import jax
import jax.numpy as jnp
import numpy as np
from jax import lax
from jax.experimental import pallas as pl
from jax.experimental.pallas import tpu as pltpu
from jax.sharding import PartitionSpec as P

DATES = 300
SPAN = 40
TIME_SIGMA = 6
RIM_WIDTH = 4

DATE_ROWS = 304
DATE_LANES = 384

IFG_COUNT = 32
BAND_COUNT = 16
OWN_IFGS = 48
ROWS = 6
COLS = 48
PIXELS = ROWS * COLS
IFGS = IFG_COUNT * OWN_IFGS

WIDE = COLS + 2 * RIM_WIDTH
WIDE_PIXELS = ROWS * WIDE
LANES = 384

GROUP = 16
GROUPS = OWN_IFGS // GROUP
TAIL = WIDE_PIXELS - 256
SPARE = 128 - TAIL
BLOCK = 2 * OWN_IFGS + 2 * GROUP
CHUNKS = 4
CHUNK = IFG_COUNT * COLS // CHUNKS
STORE = 4

EDGE_PIXELS = RIM_WIDTH * COLS
EDGE_ROWS = 2 * EDGE_PIXELS + EDGE_PIXELS // 2
MIB = 1024 * 1024
WHOLE = pl.BlockSpec(memory_space=pltpu.VMEM)
SCALARS = pl.BlockSpec(memory_space=pltpu.SMEM)


def split(value):
    high = value.astype(jnp.bfloat16)
    low = (value - high.astype(jnp.float32)).astype(jnp.bfloat16)
    return high, low


def dot(a, b):
    return jnp.dot(a, b, preferred_element_type=jnp.float32)


def full_dot(a, b):
    return jnp.dot(a, b, precision=lax.Precision.HIGHEST, preferred_element_type=jnp.float32)


def pieces(source, target, length):
    while length > 0:
        step = min(length, 128 - source % 128, 128 - target % 128)
        yield source // 128, target // 128, (target - source) % 128, target % 128, target % 128 + step
        source, target, length = source + step, target + step, length - step


def shifted(value, shift):
    return value if shift == 0 else pltpu.roll(value, shift, 1)


def tail_runs(group, source, pixel, length):
    for first, last, base in ((0, TAIL, 128 * group),) if group < 2 else ((0, SPARE, TAIL), (SPARE, TAIL, 128 + TAIL)):
        start, stop = max(pixel, first), min(pixel + length, last)
        if start < stop:
            yield source + start - pixel, base + start - first, stop - start


def needed_chunk(dest):
    last = dest * COLS + COLS + RIM_WIDTH - 1
    return min(last, IFG_COUNT * COLS - 1) // CHUNK


def pack_kernel(unwrapped_ref, mask_ref, out_ref, phase, mask, masked, block, in_sem, out_sem):
    loads = []
    for chunk in range(CHUNKS):
        at = (slice(None), slice(None), pl.ds(CHUNK * chunk, CHUNK))
        pair = (
            pltpu.make_async_copy(unwrapped_ref.at[at], phase.at[at], in_sem.at[0, chunk]),
            pltpu.make_async_copy(mask_ref.at[at], mask.at[at], in_sem.at[1, chunk]),
        )
        for load in pair:
            load.start()
        loads.append(pair)
    width = CHUNKS * CHUNK
    for row in range(ROWS):
        masked[row, :, 0:128] = jnp.zeros((OWN_IFGS, 128), jnp.float32)
        masked[row, :, 128 + width : 256 + width] = jnp.zeros((OWN_IFGS, 128), jnp.float32)
    lane = lax.broadcasted_iota(jnp.int32, (GROUP, 128), 1)

    def place(parts, rows, row, source, target, length):
        for source_tile, tile, shift, first, last in pieces(source, target, length):
            moved = shifted(masked[row, rows, 128 * source_tile : 128 * source_tile + 128], shift)
            parts[tile] = jnp.where((lane >= first) & (lane < last), moved, parts[tile])

    def fill(dest):
        tail = [jnp.zeros((GROUP, 128), jnp.float32)] * 2
        for group in range(GROUPS):
            rows = slice(GROUP * group, GROUP * (group + 1))
            main = [jnp.zeros((GROUP, 128), jnp.float32)] * 2
            for row in range(ROWS):
                source, target = 128 + dest * COLS - RIM_WIDTH, row * WIDE
                length = min(max(256 - target, 0), WIDE)
                place(main, rows, row, source, target, length)
                for run in tail_runs(group, source + length, target + length - 256, WIDE - length):
                    place(tail, rows, row, *run)
            block[dest, rows, :] = main[0]
            block[dest, OWN_IFGS + GROUP * group : OWN_IFGS + GROUP * (group + 1), :] = main[1]
        block[dest, 2 * OWN_IFGS : 2 * OWN_IFGS + GROUP, :] = tail[0]
        block[dest, 2 * OWN_IFGS + GROUP :, :] = tail[1]

    stores = []
    for chunk in range(CHUNKS):
        for load in loads[chunk]:
            load.wait()
        for row in range(ROWS):
            first = CHUNK * chunk
            values = phase[row, :, first : first + CHUNK] * mask[row, :, first : first + CHUNK].astype(jnp.float32)
            masked[row, :, 128 + first : 128 + first + CHUNK] = values
        for dest in range(IFG_COUNT):
            if needed_chunk(dest) == chunk:
                fill(dest)
                if (dest + 1) % STORE == 0:
                    at = pl.ds(dest + 1 - STORE, STORE)
                    store = pltpu.make_async_copy(block.at[at], out_ref.at[at], out_sem.at[dest // STORE])
                    store.start()
                    stores.append(store)
    for store in stores:
        store.wait()


def pack(unwrapped, component_mask):
    anywhere = pl.BlockSpec(memory_space=pl.ANY)
    columns = CHUNKS * CHUNK
    return pl.pallas_call(
        pack_kernel,
        in_specs=[anywhere] * 2,
        out_specs=anywhere,
        out_shape=jax.ShapeDtypeStruct((IFG_COUNT, BLOCK, 128), jnp.float32),
        scratch_shapes=[
            pltpu.VMEM((ROWS, OWN_IFGS, columns), jnp.float32),
            pltpu.VMEM((ROWS, OWN_IFGS, columns), jnp.int32),
            pltpu.VMEM((ROWS, OWN_IFGS, columns + 256), jnp.float32),
            pltpu.VMEM((IFG_COUNT, BLOCK, 128), jnp.float32),
            pltpu.SemaphoreType.DMA((2, CHUNKS)),
            pltpu.SemaphoreType.DMA((IFG_COUNT // STORE,)),
        ],
        compiler_params=pltpu.CompilerParams(vmem_limit_bytes=56 * MIB),
        cost_estimate=pl.CostEstimate(flops=2_000_000, bytes_accessed=5_600_000, transcendentals=0),
        name="mask_pack",
    )(unwrapped, component_mask)


def iota(shape, dim):
    return lax.broadcasted_iota(jnp.int32, shape, dim)


def one_hot(pairs, dates):
    date = iota((dates, pairs.shape[1]), 0)
    later = jnp.where(pairs[1:2, :] == date, 1.0, 0.0)
    return (later - jnp.where(pairs[0:1, :] == date, 1.0, 0.0)).astype(jnp.bfloat16)


def identity(rows, cols, first=0):
    return jnp.where(iota((rows, cols), 0) + first == iota((rows, cols), 1), 1.0, 0.0)


def eliminate(normal_ref, band_ref, lower_ref, scaled_ref):
    window = SPAN // 8 + 1
    blocks = DATE_ROWS // 8
    for tile in range(window, window + blocks):
        start = 8 * tile - SPAN
        rows = normal_ref[8 * tile : 8 * tile + 8, :]
        band_ref[8 * tile : 8 * tile + 8, :] = pltpu.roll(rows, (DATE_LANES - start) % DATE_LANES, 1)[:, :128]
    sub = iota((8, 128), 0)
    lane = iota((8, 128), 1)

    def block_step(block, carry):
        left, right = list(carry[:window]), list(carry[window:])
        pivots = jnp.zeros((8, 128), jnp.float32)
        for j in range(8):
            pivot_row = left[0][j : j + 1, :]
            right_row = right[0][j : j + 1, :]
            scale = jnp.broadcast_to(1.0 / pivot_row[:, j : j + 1], (8, 128))
            pivots = jnp.where(sub == j, scale, pivots)
            scaled_row = pivot_row * scale[0:1, :]
            scaled_right = right_row * jnp.concatenate([scale[0:1, :]] * 3, axis=1)
            for q in range(window):
                factor = jnp.broadcast_to(left[q][:, j : j + 1], (8, 128))
                if q == 0:
                    factor = jnp.where(sub > j, factor, 0.0)
                left[q] = left[q] - factor * scaled_row
                right[q] = right[q] - jnp.concatenate([factor] * 3, axis=1) * scaled_right
        at = pl.ds(pl.multiple_of(8 * block, 8), 8)
        lower_ref[at, :] = right[0]
        scaled_ref[at, :] = right[0] * jnp.concatenate([pivots] * 3, axis=1)
        entering = pl.multiple_of(8 * (block + window), 8)
        left = [jnp.where(lane < 120, pltpu.roll(part, 120, 1), 0.0) for part in left[1:]]
        left.append(band_ref[pl.ds(entering, 8), :])
        right = right[1:] + [identity(8, DATE_LANES, entering)]
        return tuple(left + right)

    left = [normal_ref[8 * q : 8 * q + 8, 0:128] for q in range(window)]
    right = [identity(8, DATE_LANES, 8 * q) for q in range(window)]
    lax.fori_loop(0, blocks, block_step, tuple(left + right))


def highpass_matrix():
    row, col = iota((DATE_ROWS, DATE_LANES), 0), iota((DATE_ROWS, DATE_LANES), 1)
    spread = (row - col).astype(jnp.float32)
    weights = jnp.exp(-spread * spread / (2.0 * TIME_SIGMA * TIME_SIGMA))
    weights = jnp.where(col < DATES, weights, 0.0)
    lowpass = weights / jnp.sum(weights, axis=1, keepdims=True)
    return jnp.where((row < DATES) & (col < DATES), identity(DATE_ROWS, DATE_LANES) - lowpass, 0.0)


def tap(offset):
    sigma = RIM_WIDTH / 2.0
    return jnp.where(jnp.abs(offset) <= RIM_WIDTH, jnp.exp(-offset * offset / (2.0 * sigma * sigma)), 0.0)


def split_three(value):
    first = value.astype(jnp.bfloat16)
    rest = value - first.astype(jnp.float32)
    second = rest.astype(jnp.bfloat16)
    return first, second, (rest - second.astype(jnp.float32)).astype(jnp.bfloat16)


def operators_kernel(pairs_ref, solve_ref, first_ref, second_ref, third_ref, normal_ref, band_ref, lower_ref, scaled_ref):
    design = one_hot(pairs_ref[...], DATE_LANES)
    normal = lax.dot_general(design, design, (((1,), (1,)), ((), ())), preferred_element_type=jnp.float32)
    normal_ref[...] = normal + identity(DATE_LANES, DATE_LANES)
    eliminate(normal_ref, band_ref, lower_ref, scaled_ref)
    solve = lax.dot_general(lower_ref[...], scaled_ref[...], (((0,), (0,)), ((), ())),
                            precision=lax.Precision.HIGHEST, preferred_element_type=jnp.float32)
    solve_ref[...] = solve[:DATE_ROWS]
    first_ref[...], second_ref[...], third_ref[...] = split_three(full_dot(highpass_matrix(), solve))


def operators(pairs):
    part = jax.ShapeDtypeStruct((DATE_ROWS, DATE_LANES), jnp.bfloat16)
    return pl.pallas_call(
        operators_kernel,
        in_specs=[WHOLE],
        out_specs=[WHOLE] * 4,
        out_shape=[jax.ShapeDtypeStruct((DATE_ROWS, DATE_LANES), jnp.float32)] + [part] * 3,
        scratch_shapes=[
            pltpu.VMEM((DATE_LANES, DATE_LANES), jnp.float32),
            pltpu.VMEM((DATE_LANES, 128), jnp.float32),
            pltpu.VMEM((DATE_ROWS, DATE_LANES), jnp.float32),
            pltpu.VMEM((DATE_ROWS, DATE_LANES), jnp.float32),
        ],
        compiler_params=pltpu.CompilerParams(vmem_limit_bytes=24 * MIB),
        cost_estimate=pl.CostEstimate(flops=20_000_000_000, bytes_accessed=3_000_000, transcendentals=0),
        name="operators",
    )(pairs)


def padded(value):
    return jnp.concatenate([value, jnp.zeros((DATE_LANES - DATE_ROWS, LANES), jnp.float32)], axis=0)


def gather_dates(ordered_ref, data_ref):
    def block(start):
        return split(data_ref[:, start : start + GROUP, :].reshape(GROUP * IFG_COUNT, 128))

    tails = [block(2 * OWN_IFGS), block(2 * OWN_IFGS + GROUP)]
    main, rest, spare = None, None, None
    for group in range(GROUPS):
        parts = [block(GROUP * group), block(OWN_IFGS + GROUP * group)]
        parts += tails if group == 2 else [tails[group]]
        design = one_hot(ordered_ref[:, 512 * group : 512 * group + 512], DATE_ROWS)
        high = jnp.concatenate([part[0] for part in parts], axis=1)
        low = jnp.concatenate([part[1] for part in parts], axis=1)
        sums = dot(design, high) + dot(design, low)
        main = sums[:, :256] if main is None else main + sums[:, :256]
        if group == 2:
            spare = sums[:, 256:]
        else:
            rest = sums[:, 256:] if rest is None else rest + sums[:, 256:]
    lane = iota((DATE_ROWS, 128), 1)
    first, second = shifted(spare[:, :128], 128 - TAIL), shifted(spare[:, 128:], 128 - TAIL + SPARE)
    rest = jnp.where(lane < TAIL, rest + jnp.where(lane < SPARE, first, second), 0.0)
    return jnp.concatenate([main, rest], axis=1)


def weight(offset):
    sigma = RIM_WIDTH / 2.0
    return float(np.exp(-offset * offset / (2.0 * sigma * sigma)))


def send_edge(edge_ref, own_ref, first):
    half = RIM_WIDTH // 2
    lane = iota((COLS, 128), 1)

    def own(place, tile):
        start = COLS * (first + place)
        return own_ref[start : start + COLS, 128 * tile : 128 * (tile + 1)]

    for place in range(RIM_WIDTH):
        for tile in range(2):
            start = EDGE_PIXELS * tile + COLS * place
            edge_ref[start : start + COLS, :] = own(place, tile)
    for place in range(half):
        start = 2 * EDGE_PIXELS + COLS * place
        edge_ref[start : start + COLS, :] = jnp.where(lane < 64, own(place, 2), pltpu.roll(own(place + half, 2), 64, 1))


def varying_kernel(core_ref, ordered_ref, data_ref, first_ref, second_ref, third_ref, scale_ref, sums_ref, own_ref,
                   edge_a_ref, edge_b_ref, wide_ref):
    sums = padded(gather_dates(ordered_ref, data_ref))
    sums_ref[...] = sums
    left = [first_ref[...], second_ref[...], third_ref[...]]
    right = split_three(sums)
    orders = ((2, 0), (0, 2), (1, 1), (1, 0), (0, 1), (0, 0))
    varying = dot(
        jnp.concatenate([left[i] for i, _ in orders], axis=1), jnp.concatenate([right[j] for _, j in orders], axis=0)
    )
    varying = padded(varying).T
    for tile in range(3):
        wide_ref[tile] = varying[:, 128 * tile : 128 * (tile + 1)]
        for row in range(ROWS):
            start = WIDE * row + RIM_WIDTH
            total = wide_ref[tile, start : start + COLS, :]
            for offset in range(1, RIM_WIDTH + 1):
                both = wide_ref[tile, start - offset : start - offset + COLS, :]
                both = both + wide_ref[tile, start + offset : start + offset + COLS, :]
                total = total + weight(offset) * both
            own_ref[COLS * row : COLS * (row + 1), 128 * tile : 128 * (tile + 1)] = total * scale_ref[...]
    for core, (edge_down, edge_up) in enumerate(((edge_a_ref, edge_b_ref), (edge_b_ref, edge_a_ref))):

        @pl.when(core_ref[0] == core)
        def _():
            send_edge(edge_down, own_ref, ROWS - RIM_WIDTH)
            send_edge(edge_up, own_ref, 0)


def project_varying(core, ordered, data, filtered, column_scale):
    edge = jax.ShapeDtypeStruct((EDGE_ROWS, 128), jnp.float32)
    return pl.pallas_call(
        varying_kernel,
        in_specs=[SCALARS] + [WHOLE] * 6,
        out_specs=[WHOLE] * 4,
        out_shape=[
            jax.ShapeDtypeStruct((DATE_LANES, LANES), jnp.float32),
            jax.ShapeDtypeStruct((PIXELS, DATE_LANES), jnp.float32),
            edge,
            edge,
        ],
        scratch_shapes=[pltpu.VMEM((3, LANES, 128), jnp.float32)],
        compiler_params=pltpu.CompilerParams(vmem_limit_bytes=24 * MIB),
        cost_estimate=pl.CostEstimate(flops=1_100_000_000, bytes_accessed=5_000_000, transcendentals=0),
        name="varying",
    )(core, ordered, data, *filtered, column_scale)


def series_kernel(scale_ref, solve_ref, sums_ref, smooth_ref, series_ref, partial_ref):
    series = padded(full_dot(solve_ref[...], sums_ref[...])).T
    for row in range(ROWS):
        start = WIDE * row + RIM_WIDTH
        own = series[start : start + COLS]
        series_ref[row] = own[:, :DATES]
        total = None
        for other in range(ROWS):
            if abs(other - row) <= RIM_WIDTH:
                term = weight(other - row) * smooth_ref[COLS * other : COLS * (other + 1), :]
                total = term if total is None else total + term
        partial_ref[COLS * row : COLS * (row + 1), :] = own - total * scale_ref[row]


def project_series(row_scale, solve, sums, smooth):
    return pl.pallas_call(
        series_kernel,
        in_specs=[SCALARS] + [WHOLE] * 3,
        out_specs=[WHOLE] * 2,
        out_shape=[
            jax.ShapeDtypeStruct((ROWS, COLS, DATES), jnp.float32),
            jax.ShapeDtypeStruct((PIXELS, DATE_LANES), jnp.float32),
        ],
        compiler_params=pltpu.CompilerParams(vmem_limit_bytes=16 * MIB),
        cost_estimate=pl.CostEstimate(flops=2_000_000_000, bytes_accessed=2_000_000, transcendentals=0),
        name="series",
    )(row_scale, solve, sums, smooth)


def edge_tile(edge_ref, row, tile):
    if tile < 2:
        start = EDGE_PIXELS * tile + COLS * row
        return edge_ref[start : start + COLS, :]
    start = 2 * EDGE_PIXELS + COLS * (row % 2)
    return shifted(edge_ref[start : start + COLS, :], 64 * (row // 2))


def corrected_kernel(core_ref, scale_ref, partial_ref, edge_a_ref, edge_b_ref, out_ref):
    for core, (above_ref, below_ref) in enumerate(((edge_a_ref, edge_b_ref), (edge_b_ref, edge_a_ref))):

        @pl.when(core_ref[0] == core)
        def _():
            for row in range(ROWS):
                near = [(other - RIM_WIDTH - row, above_ref, other) for other in range(RIM_WIDTH)]
                near += [(ROWS + other - row, below_ref, other) for other in range(RIM_WIDTH)]
                near = [entry for entry in near if abs(entry[0]) <= RIM_WIDTH]
                for tile in range(3):
                    total = sum(weight(offset) * edge_tile(ref, other, tile) for offset, ref, other in near)
                    part = partial_ref[COLS * row : COLS * (row + 1), 128 * tile : 128 * (tile + 1)]
                    width = min(128, DATES - 128 * tile)
                    out_ref[row, :, 128 * tile : 128 * tile + width] = (part - total * scale_ref[row])[:, :width]


def correct(core, row_scale, partial, edge_a, edge_b):
    return pl.pallas_call(
        corrected_kernel,
        in_specs=[SCALARS] * 2 + [WHOLE] * 3,
        out_specs=WHOLE,
        out_shape=jax.ShapeDtypeStruct((ROWS, COLS, DATES), jnp.float32),
        compiler_params=pltpu.CompilerParams(vmem_limit_bytes=16 * MIB),
        cost_estimate=pl.CostEstimate(flops=1_000_000, bytes_accessed=1_400_000, transcendentals=0),
        name="corrected",
    )(core, row_scale, partial, edge_a, edge_b)


def pass_on(edge, first_way):
    pairs = []
    for i in range(IFG_COUNT):
        way = first_way if i % 2 == 0 else -first_way
        for b in range(BAND_COUNT):
            if 0 <= b + way < BAND_COUNT:
                pairs.append((i * BAND_COUNT + b, i * BAND_COUNT + b + way))
    return lax.ppermute(edge, ("ifg", "band"), pairs)


def edge_weights(start, count, total):
    offsets = jnp.arange(-RIM_WIDTH, RIM_WIDTH + 1, dtype=jnp.int32)
    places = start + jnp.arange(count, dtype=jnp.int32)[:, None] + offsets[None, :]
    inside = ((places >= 0) & (places < total)).astype(jnp.float32)
    return jnp.sum(inside * tap(offsets.astype(jnp.float32))[None, :], axis=1)


def body(unwrapped, component_mask, date_pairs):
    blocks = pack(unwrapped.transpose(1, 0, 2), component_mask.transpose(1, 0, 2))
    data = lax.all_to_all(blocks, "ifg", split_axis=0, concat_axis=0, tiled=True)
    row_scale = 1.0 / edge_weights(lax.axis_index("band") * ROWS, ROWS, ROWS * BAND_COUNT)
    column_norm = edge_weights(lax.axis_index("ifg") * COLS, COLS, COLS * IFG_COUNT)
    pairs = date_pairs.T
    ordered = pairs.reshape(2, IFG_COUNT, GROUPS, GROUP).transpose(0, 2, 1, 3).reshape(2, IFGS)
    column_scale = jnp.broadcast_to((1.0 / column_norm)[:, None], (COLS, 128))
    solve, *filtered = operators(pairs)
    core = (lax.axis_index("ifg") % 2)[None]
    sums, smooth, edge_a, edge_b = project_varying(core, ordered, data, filtered, column_scale)
    edge_a, edge_b = pass_on(edge_a, 1), pass_on(edge_b, -1)
    series, partial = project_series(row_scale, solve, sums, smooth)
    corrected = correct(core, row_scale, partial, edge_a, edge_b)
    return series.transpose(2, 0, 1), corrected.transpose(2, 0, 1)


def solution(mesh):
    placed = (P("ifg", "band", None), P("ifg", "band", None), P())
    return jax.shard_map(
        body,
        mesh=mesh,
        in_specs=placed,
        out_specs=(P(None, "band", "ifg"), P(None, "band", "ifg")),
        check_vma=False,
    )
```

```python
import jax
import jax.numpy as jnp
import numpy as np
from jax import lax
from jax.experimental import pallas as pl
from jax.experimental.pallas import tpu as pltpu
from jax.sharding import PartitionSpec as P

DATES = 300
SPAN = 40
TIME_SIGMA = 6
RIM_WIDTH = 4

DATE_ROWS = 304
DATE_LANES = 384

IFG_COUNT = 32
BAND_COUNT = 16
OWN_IFGS = 48
ROWS = 6
COLS = 48
PIXELS = ROWS * COLS
IFGS = IFG_COUNT * OWN_IFGS

WIDE = COLS + 2 * RIM_WIDTH
WIDE_PIXELS = ROWS * WIDE
LANES = 384

GROUP = 16
GROUPS = OWN_IFGS // GROUP
TAIL = WIDE_PIXELS - 256
SPARE = 128 - TAIL
BLOCK = 2 * OWN_IFGS + 2 * GROUP
CHUNKS = 4
CHUNK = IFG_COUNT * COLS // CHUNKS
STORE = 4

EDGE_PIXELS = RIM_WIDTH * COLS
EDGE_ROWS = 2 * EDGE_PIXELS + EDGE_PIXELS // 2
MIB = 1024 * 1024
WHOLE = pl.BlockSpec(memory_space=pltpu.VMEM)


def split(value):
    high = value.astype(jnp.bfloat16)
    low = (value - high.astype(jnp.float32)).astype(jnp.bfloat16)
    return high, low


def dot(a, b):
    return jnp.dot(a, b, preferred_element_type=jnp.float32)


def full_dot(a, b):
    return jnp.dot(a, b, precision=lax.Precision.HIGHEST, preferred_element_type=jnp.float32)


def pieces(source, target, length):
    while length > 0:
        step = min(length, 128 - source % 128, 128 - target % 128)
        yield source // 128, target // 128, (target - source) % 128, target % 128, target % 128 + step
        source, target, length = source + step, target + step, length - step


def shifted(value, shift):
    return value if shift == 0 else pltpu.roll(value, shift, 1)


def tail_runs(group, source, pixel, length):
    for first, last, base in ((0, TAIL, 128 * group),) if group < 2 else ((0, SPARE, TAIL), (SPARE, TAIL, 128 + TAIL)):
        start, stop = max(pixel, first), min(pixel + length, last)
        if start < stop:
            yield source + start - pixel, base + start - first, stop - start


def needed_chunk(dest):
    last = dest * COLS + COLS + RIM_WIDTH - 1
    return min(last, IFG_COUNT * COLS - 1) // CHUNK


def pack_kernel(unwrapped_ref, mask_ref, out_ref, phase, mask, masked, block, in_sem, out_sem):
    loads = []
    for chunk in range(CHUNKS):
        at = (slice(None), slice(None), pl.ds(CHUNK * chunk, CHUNK))
        pair = (
            pltpu.make_async_copy(unwrapped_ref.at[at], phase.at[at], in_sem.at[0, chunk]),
            pltpu.make_async_copy(mask_ref.at[at], mask.at[at], in_sem.at[1, chunk]),
        )
        for load in pair:
            load.start()
        loads.append(pair)
    width = CHUNKS * CHUNK
    for row in range(ROWS):
        masked[row, :, 0:128] = jnp.zeros((OWN_IFGS, 128), jnp.float32)
        masked[row, :, 128 + width : 256 + width] = jnp.zeros((OWN_IFGS, 128), jnp.float32)
    lane = lax.broadcasted_iota(jnp.int32, (GROUP, 128), 1)

    def place(parts, rows, row, source, target, length):
        for source_tile, tile, shift, first, last in pieces(source, target, length):
            moved = shifted(masked[row, rows, 128 * source_tile : 128 * source_tile + 128], shift)
            parts[tile] = jnp.where((lane >= first) & (lane < last), moved, parts[tile])

    def fill(dest):
        tail = [jnp.zeros((GROUP, 128), jnp.float32)] * 2
        for group in range(GROUPS):
            rows = slice(GROUP * group, GROUP * (group + 1))
            main = [jnp.zeros((GROUP, 128), jnp.float32)] * 2
            for row in range(ROWS):
                source, target = 128 + dest * COLS - RIM_WIDTH, row * WIDE
                length = min(max(256 - target, 0), WIDE)
                place(main, rows, row, source, target, length)
                for run in tail_runs(group, source + length, target + length - 256, WIDE - length):
                    place(tail, rows, row, *run)
            block[dest, rows, :] = main[0]
            block[dest, OWN_IFGS + GROUP * group : OWN_IFGS + GROUP * (group + 1), :] = main[1]
        block[dest, 2 * OWN_IFGS : 2 * OWN_IFGS + GROUP, :] = tail[0]
        block[dest, 2 * OWN_IFGS + GROUP :, :] = tail[1]

    stores = []
    for chunk in range(CHUNKS):
        for load in loads[chunk]:
            load.wait()
        for row in range(ROWS):
            first = CHUNK * chunk
            values = phase[row, :, first : first + CHUNK] * mask[row, :, first : first + CHUNK].astype(jnp.float32)
            masked[row, :, 128 + first : 128 + first + CHUNK] = values
        for dest in range(IFG_COUNT):
            if needed_chunk(dest) == chunk:
                fill(dest)
                if (dest + 1) % STORE == 0:
                    at = pl.ds(dest + 1 - STORE, STORE)
                    store = pltpu.make_async_copy(block.at[at], out_ref.at[at], out_sem.at[dest // STORE])
                    store.start()
                    stores.append(store)
    for store in stores:
        store.wait()


def pack(unwrapped, component_mask):
    anywhere = pl.BlockSpec(memory_space=pl.ANY)
    columns = CHUNKS * CHUNK
    return pl.pallas_call(
        pack_kernel,
        in_specs=[anywhere] * 2,
        out_specs=anywhere,
        out_shape=jax.ShapeDtypeStruct((IFG_COUNT, BLOCK, 128), jnp.float32),
        scratch_shapes=[
            pltpu.VMEM((ROWS, OWN_IFGS, columns), jnp.float32),
            pltpu.VMEM((ROWS, OWN_IFGS, columns), jnp.int32),
            pltpu.VMEM((ROWS, OWN_IFGS, columns + 256), jnp.float32),
            pltpu.VMEM((IFG_COUNT, BLOCK, 128), jnp.float32),
            pltpu.SemaphoreType.DMA((2, CHUNKS)),
            pltpu.SemaphoreType.DMA((IFG_COUNT // STORE,)),
        ],
        compiler_params=pltpu.CompilerParams(vmem_limit_bytes=56 * MIB),
        cost_estimate=pl.CostEstimate(flops=2_000_000, bytes_accessed=5_600_000, transcendentals=0),
        name="mask_pack",
    )(unwrapped, component_mask)


def iota(shape, dim):
    return lax.broadcasted_iota(jnp.int32, shape, dim)


def one_hot(pairs, dates):
    date = iota((dates, pairs.shape[1]), 0)
    later = jnp.where(pairs[1:2, :] == date, 1.0, 0.0)
    return (later - jnp.where(pairs[0:1, :] == date, 1.0, 0.0)).astype(jnp.bfloat16)


def identity(rows, cols, first=0):
    return jnp.where(iota((rows, cols), 0) + first == iota((rows, cols), 1), 1.0, 0.0)


def eliminate(normal_ref, band_ref, lower_ref, scaled_ref):
    window = SPAN // 8 + 1
    blocks = DATE_ROWS // 8
    for tile in range(window, window + blocks):
        start = 8 * tile - SPAN
        rows = normal_ref[8 * tile : 8 * tile + 8, :]
        band_ref[8 * tile : 8 * tile + 8, :] = pltpu.roll(rows, (DATE_LANES - start) % DATE_LANES, 1)[:, :128]
    sub = iota((8, 128), 0)
    lane = iota((8, 128), 1)

    def block_step(block, carry):
        left, right = list(carry[:window]), list(carry[window:])
        pivots = jnp.zeros((8, 128), jnp.float32)
        for j in range(8):
            pivot_row = left[0][j : j + 1, :]
            right_row = right[0][j : j + 1, :]
            scale = jnp.broadcast_to(1.0 / pivot_row[:, j : j + 1], (8, 128))
            pivots = jnp.where(sub == j, scale, pivots)
            scaled_row = pivot_row * scale[0:1, :]
            scaled_right = right_row * jnp.concatenate([scale[0:1, :]] * 3, axis=1)
            for q in range(window):
                factor = jnp.broadcast_to(left[q][:, j : j + 1], (8, 128))
                if q == 0:
                    factor = jnp.where(sub > j, factor, 0.0)
                left[q] = left[q] - factor * scaled_row
                right[q] = right[q] - jnp.concatenate([factor] * 3, axis=1) * scaled_right
        at = pl.ds(pl.multiple_of(8 * block, 8), 8)
        lower_ref[at, :] = right[0]
        scaled_ref[at, :] = right[0] * jnp.concatenate([pivots] * 3, axis=1)
        entering = pl.multiple_of(8 * (block + window), 8)
        left = [jnp.where(lane < 120, pltpu.roll(part, 120, 1), 0.0) for part in left[1:]]
        left.append(band_ref[pl.ds(entering, 8), :])
        right = right[1:] + [identity(8, DATE_LANES, entering)]
        return tuple(left + right)

    left = [normal_ref[8 * q : 8 * q + 8, 0:128] for q in range(window)]
    right = [identity(8, DATE_LANES, 8 * q) for q in range(window)]
    lax.fori_loop(0, blocks, block_step, tuple(left + right))


def highpass_matrix():
    row, col = iota((DATE_ROWS, DATE_LANES), 0), iota((DATE_ROWS, DATE_LANES), 1)
    spread = (row - col).astype(jnp.float32)
    weights = jnp.exp(-spread * spread / (2.0 * TIME_SIGMA * TIME_SIGMA))
    weights = jnp.where(col < DATES, weights, 0.0)
    lowpass = weights / jnp.sum(weights, axis=1, keepdims=True)
    return jnp.where((row < DATES) & (col < DATES), identity(DATE_ROWS, DATE_LANES) - lowpass, 0.0)


def tap(offset):
    sigma = RIM_WIDTH / 2.0
    return jnp.where(jnp.abs(offset) <= RIM_WIDTH, jnp.exp(-offset * offset / (2.0 * sigma * sigma)), 0.0)


def split_three(value):
    first = value.astype(jnp.bfloat16)
    rest = value - first.astype(jnp.float32)
    second = rest.astype(jnp.bfloat16)
    return first, second, (rest - second.astype(jnp.float32)).astype(jnp.bfloat16)


def operators_kernel(pairs_ref, solve_ref, first_ref, second_ref, third_ref, normal_ref, band_ref, lower_ref, scaled_ref):
    design = one_hot(pairs_ref[...], DATE_LANES)
    normal = lax.dot_general(design, design, (((1,), (1,)), ((), ())), preferred_element_type=jnp.float32)
    normal_ref[...] = normal + identity(DATE_LANES, DATE_LANES)
    eliminate(normal_ref, band_ref, lower_ref, scaled_ref)
    solve = lax.dot_general(lower_ref[...], scaled_ref[...], (((0,), (0,)), ((), ())),
                            precision=lax.Precision.HIGHEST, preferred_element_type=jnp.float32)
    solve_ref[...] = solve[:DATE_ROWS]
    first_ref[...], second_ref[...], third_ref[...] = split_three(full_dot(highpass_matrix(), solve))


def operators(pairs):
    part = jax.ShapeDtypeStruct((DATE_ROWS, DATE_LANES), jnp.bfloat16)
    return pl.pallas_call(
        operators_kernel,
        in_specs=[WHOLE],
        out_specs=[WHOLE] * 4,
        out_shape=[jax.ShapeDtypeStruct((DATE_ROWS, DATE_LANES), jnp.float32)] + [part] * 3,
        scratch_shapes=[
            pltpu.VMEM((DATE_LANES, DATE_LANES), jnp.float32),
            pltpu.VMEM((DATE_LANES, 128), jnp.float32),
            pltpu.VMEM((DATE_ROWS, DATE_LANES), jnp.float32),
            pltpu.VMEM((DATE_ROWS, DATE_LANES), jnp.float32),
        ],
        compiler_params=pltpu.CompilerParams(vmem_limit_bytes=24 * MIB),
        cost_estimate=pl.CostEstimate(flops=20_000_000_000, bytes_accessed=3_000_000, transcendentals=0),
        name="operators",
    )(pairs)


def padded(value):
    return jnp.concatenate([value, jnp.zeros((DATE_LANES - DATE_ROWS, LANES), jnp.float32)], axis=0)


def gather_dates(ordered_ref, data_ref):
    def block(start):
        return split(data_ref[:, start : start + GROUP, :].reshape(GROUP * IFG_COUNT, 128))

    tails = [block(2 * OWN_IFGS), block(2 * OWN_IFGS + GROUP)]
    main, rest, spare = None, None, None
    for group in range(GROUPS):
        parts = [block(GROUP * group), block(OWN_IFGS + GROUP * group)]
        parts += tails if group == 2 else [tails[group]]
        design = one_hot(ordered_ref[:, 512 * group : 512 * group + 512], DATE_ROWS)
        high = jnp.concatenate([part[0] for part in parts], axis=1)
        low = jnp.concatenate([part[1] for part in parts], axis=1)
        sums = dot(design, high) + dot(design, low)
        main = sums[:, :256] if main is None else main + sums[:, :256]
        if group == 2:
            spare = sums[:, 256:]
        else:
            rest = sums[:, 256:] if rest is None else rest + sums[:, 256:]
    lane = iota((DATE_ROWS, 128), 1)
    first, second = shifted(spare[:, :128], 128 - TAIL), shifted(spare[:, 128:], 128 - TAIL + SPARE)
    rest = jnp.where(lane < TAIL, rest + jnp.where(lane < SPARE, first, second), 0.0)
    return jnp.concatenate([main, rest], axis=1)


def weight(offset):
    sigma = RIM_WIDTH / 2.0
    return float(np.exp(-offset * offset / (2.0 * sigma * sigma)))


def send_edge(edge_ref, own_ref, first):
    half = RIM_WIDTH // 2
    lane = iota((COLS, 128), 1)

    def own(place, tile):
        start = COLS * (first + place)
        return own_ref[start : start + COLS, 128 * tile : 128 * (tile + 1)]

    for place in range(RIM_WIDTH):
        for tile in range(2):
            start = EDGE_PIXELS * tile + COLS * place
            edge_ref[start : start + COLS, :] = own(place, tile)
    for place in range(half):
        start = 2 * EDGE_PIXELS + COLS * place
        edge_ref[start : start + COLS, :] = jnp.where(lane < 64, own(place, 2), pltpu.roll(own(place + half, 2), 64, 1))


def varying_kernel(ordered_ref, data_ref, first_ref, second_ref, third_ref, scale_ref, sums_ref, own_ref,
                   edge_a_ref, edge_b_ref, wide_ref):
    sums = padded(gather_dates(ordered_ref, data_ref))
    sums_ref[...] = sums
    left = [first_ref[...], second_ref[...], third_ref[...]]
    right = split_three(sums)
    orders = ((2, 0), (0, 2), (1, 1), (1, 0), (0, 1), (0, 0))
    varying = dot(
        jnp.concatenate([left[i] for i, _ in orders], axis=1), jnp.concatenate([right[j] for _, j in orders], axis=0)
    )
    varying = padded(varying).T
    for tile in range(3):
        wide_ref[tile] = varying[:, 128 * tile : 128 * (tile + 1)]
        for row in range(ROWS):
            start = WIDE * row + RIM_WIDTH
            total = wide_ref[tile, start : start + COLS, :]
            for offset in range(1, RIM_WIDTH + 1):
                both = wide_ref[tile, start - offset : start - offset + COLS, :]
                both = both + wide_ref[tile, start + offset : start + offset + COLS, :]
                total = total + weight(offset) * both
            own_ref[COLS * row : COLS * (row + 1), 128 * tile : 128 * (tile + 1)] = total * scale_ref[...]
    for core, (edge_down, edge_up) in enumerate(((edge_a_ref, edge_b_ref), (edge_b_ref, edge_a_ref))):

        @pl.when(lax.axis_index("ifg") % 2 == core)
        def _():
            send_edge(edge_down, own_ref, ROWS - RIM_WIDTH)
            send_edge(edge_up, own_ref, 0)


def project_varying(ordered, data, filtered, column_scale):
    edge = jax.ShapeDtypeStruct((EDGE_ROWS, 128), jnp.float32)
    return pl.pallas_call(
        varying_kernel,
        in_specs=[WHOLE] * 6,
        out_specs=[WHOLE] * 4,
        out_shape=[
            jax.ShapeDtypeStruct((DATE_LANES, LANES), jnp.float32),
            jax.ShapeDtypeStruct((PIXELS, DATE_LANES), jnp.float32),
            edge,
            edge,
        ],
        scratch_shapes=[pltpu.VMEM((3, LANES, 128), jnp.float32)],
        compiler_params=pltpu.CompilerParams(vmem_limit_bytes=24 * MIB),
        cost_estimate=pl.CostEstimate(flops=1_100_000_000, bytes_accessed=5_000_000, transcendentals=0),
        name="varying",
    )(ordered, data, *filtered, column_scale)


def series_kernel(scale_ref, solve_ref, sums_ref, smooth_ref, series_ref, partial_ref):
    series = padded(full_dot(solve_ref[...], sums_ref[...])).T
    for row in range(ROWS):
        start = WIDE * row + RIM_WIDTH
        own = series[start : start + COLS]
        series_ref[row] = own[:, :DATES]
        total = None
        for other in range(ROWS):
            if abs(other - row) <= RIM_WIDTH:
                term = weight(other - row) * smooth_ref[COLS * other : COLS * (other + 1), :]
                total = term if total is None else total + term
        partial_ref[COLS * row : COLS * (row + 1), :] = own - total * jnp.concatenate([scale_ref[row : row + 1, :]] * 3, axis=1)


def project_series(row_scale, solve, sums, smooth):
    return pl.pallas_call(
        series_kernel,
        in_specs=[WHOLE] * 4,
        out_specs=[WHOLE] * 2,
        out_shape=[
            jax.ShapeDtypeStruct((ROWS, COLS, DATES), jnp.float32),
            jax.ShapeDtypeStruct((PIXELS, DATE_LANES), jnp.float32),
        ],
        compiler_params=pltpu.CompilerParams(vmem_limit_bytes=16 * MIB),
        cost_estimate=pl.CostEstimate(flops=2_000_000_000, bytes_accessed=2_000_000, transcendentals=0),
        name="series",
    )(row_scale, solve, sums, smooth)


def edge_tile(edge_ref, row, tile):
    if tile < 2:
        start = EDGE_PIXELS * tile + COLS * row
        return edge_ref[start : start + COLS, :]
    start = 2 * EDGE_PIXELS + COLS * (row % 2)
    return shifted(edge_ref[start : start + COLS, :], 64 * (row // 2))


def corrected_kernel(scale_ref, partial_ref, edge_a_ref, edge_b_ref, out_ref):
    for core, (above_ref, below_ref) in enumerate(((edge_a_ref, edge_b_ref), (edge_b_ref, edge_a_ref))):

        @pl.when(lax.axis_index("ifg") % 2 == core)
        def _():
            for row in range(ROWS):
                near = [(other - RIM_WIDTH - row, above_ref, other) for other in range(RIM_WIDTH)]
                near += [(ROWS + other - row, below_ref, other) for other in range(RIM_WIDTH)]
                near = [entry for entry in near if abs(entry[0]) <= RIM_WIDTH]
                scale = scale_ref[row : row + 1, :]
                for tile in range(3):
                    total = sum(weight(offset) * edge_tile(ref, other, tile) for offset, ref, other in near)
                    part = partial_ref[COLS * row : COLS * (row + 1), 128 * tile : 128 * (tile + 1)]
                    width = min(128, DATES - 128 * tile)
                    out_ref[row, :, 128 * tile : 128 * tile + width] = (part - total * scale)[:, :width]


def correct(row_scale, partial, edge_a, edge_b):
    return pl.pallas_call(
        corrected_kernel,
        in_specs=[WHOLE] * 4,
        out_specs=WHOLE,
        out_shape=jax.ShapeDtypeStruct((ROWS, COLS, DATES), jnp.float32),
        compiler_params=pltpu.CompilerParams(vmem_limit_bytes=16 * MIB),
        cost_estimate=pl.CostEstimate(flops=1_000_000, bytes_accessed=1_400_000, transcendentals=0),
        name="corrected",
    )(row_scale, partial, edge_a, edge_b)


def pass_on(edge, first_way):
    pairs = []
    for i in range(IFG_COUNT):
        way = first_way if i % 2 == 0 else -first_way
        for b in range(BAND_COUNT):
            if 0 <= b + way < BAND_COUNT:
                pairs.append((i * BAND_COUNT + b, i * BAND_COUNT + b + way))
    return lax.ppermute(edge, ("ifg", "band"), pairs)


def edge_weights(start, count, total):
    offsets = jnp.arange(-RIM_WIDTH, RIM_WIDTH + 1, dtype=jnp.int32)
    places = start + jnp.arange(count, dtype=jnp.int32)[:, None] + offsets[None, :]
    inside = ((places >= 0) & (places < total)).astype(jnp.float32)
    return jnp.sum(inside * tap(offsets.astype(jnp.float32))[None, :], axis=1)


def body(unwrapped, component_mask, date_pairs):
    blocks = pack(unwrapped.transpose(1, 0, 2), component_mask.transpose(1, 0, 2))
    data = lax.all_to_all(blocks, "ifg", split_axis=0, concat_axis=0, tiled=True)
    row_norm = edge_weights(lax.axis_index("band") * ROWS, ROWS, ROWS * BAND_COUNT)
    row_scale = jnp.broadcast_to((1.0 / row_norm)[:, None], (ROWS, 128))
    column_norm = edge_weights(lax.axis_index("ifg") * COLS, COLS, COLS * IFG_COUNT)
    pairs = date_pairs.T
    ordered = pairs.reshape(2, IFG_COUNT, GROUPS, GROUP).transpose(0, 2, 1, 3).reshape(2, IFGS)
    column_scale = jnp.broadcast_to((1.0 / column_norm)[:, None], (COLS, 128))
    solve, *filtered = operators(pairs)
    sums, smooth, edge_a, edge_b = project_varying(ordered, data, filtered, column_scale)
    edge_a, edge_b = pass_on(edge_a, 1), pass_on(edge_b, -1)
    series, partial = project_series(row_scale, solve, sums, smooth)
    corrected = correct(row_scale, partial, edge_a, edge_b)
    return series.transpose(2, 0, 1), corrected.transpose(2, 0, 1)


def solution(mesh):
    placed = (P("ifg", "band", None), P("ifg", "band", None), P())
    return jax.shard_map(
        body,
        mesh=mesh,
        in_specs=placed,
        out_specs=(P(None, "band", "ifg"), P(None, "band", "ifg")),
        check_vma=False,
    )
```

```python
import jax
import jax.numpy as jnp
import numpy as np
from jax import lax
from jax.experimental import pallas as pl
from jax.experimental.pallas import tpu as pltpu
from jax.sharding import PartitionSpec as P

DATES = 300
SPAN = 40
TIME_SIGMA = 6
RIM_WIDTH = 4

DATE_ROWS = 304
DATE_LANES = 384

IFG_COUNT = 32
BAND_COUNT = 16
OWN_IFGS = 48
ROWS = 6
COLS = 48
PIXELS = ROWS * COLS
IFGS = IFG_COUNT * OWN_IFGS

WIDE = COLS + 2 * RIM_WIDTH
WIDE_PIXELS = ROWS * WIDE
LANES = 384

GROUP = 16
GROUPS = OWN_IFGS // GROUP
TAIL = WIDE_PIXELS - 256
SPARE = 128 - TAIL
BLOCK = 2 * OWN_IFGS + 2 * GROUP
CHUNKS = 4
CHUNK = IFG_COUNT * COLS // CHUNKS
STORE = 4

EDGE_PIXELS = RIM_WIDTH * COLS
EDGE_ROWS = 2 * EDGE_PIXELS + EDGE_PIXELS // 2
MIB = 1024 * 1024
WHOLE = pl.BlockSpec(memory_space=pltpu.VMEM)


def split(value):
    high = value.astype(jnp.bfloat16)
    low = (value - high.astype(jnp.float32)).astype(jnp.bfloat16)
    return high, low


def dot(a, b):
    return jnp.dot(a, b, preferred_element_type=jnp.float32)


def full_dot(a, b):
    return jnp.dot(a, b, precision=lax.Precision.HIGHEST, preferred_element_type=jnp.float32)


def shifted(value, shift):
    return value if shift == 0 else pltpu.roll(value, shift, 1)


def needed_chunk(dest):
    last = dest * COLS + COLS + RIM_WIDTH - 1
    return min(last, IFG_COUNT * COLS - 1) // CHUNK


def pack_kernel(unwrapped_ref, mask_ref, out_ref, phase, mask, masked, block, in_sem, out_sem):
    loads = []
    for chunk in range(CHUNKS):
        at = (slice(None), slice(None), pl.ds(CHUNK * chunk, CHUNK))
        pair = (
            pltpu.make_async_copy(unwrapped_ref.at[at], phase.at[at], in_sem.at[0, chunk]),
            pltpu.make_async_copy(mask_ref.at[at], mask.at[at], in_sem.at[1, chunk]),
        )
        for load in pair:
            load.start()
        loads.append(pair)
    width = CHUNKS * CHUNK
    for row in range(ROWS):
        masked[row, :, 0:128] = jnp.zeros((OWN_IFGS, 128), jnp.float32)
        masked[row, :, 128 + width : 256 + width] = jnp.zeros((OWN_IFGS, 128), jnp.float32)
    lane = lax.broadcasted_iota(jnp.int32, (GROUP, 128), 1)

    def fill(dest):
        source_tile, start = divmod(128 + dest * COLS - RIM_WIDTH, 128)
        tail = [None] * 2
        for group in range(GROUPS):
            rows = slice(GROUP * group, GROUP * (group + 1))
            main = [None] * 2

            def put(parts, tile, first, moved):
                parts[tile] = moved if first == 0 else jnp.where(lane >= first, moved, parts[tile])

            for row in range(ROWS):
                run = masked[row, rows, 128 * source_tile : 128 * source_tile + 128]
                if start + WIDE > 128:
                    rest = masked[row, rows, 128 * source_tile + 128 : 128 * source_tile + 256]
                    run = jnp.where(lane >= start, run, rest)
                target = row * WIDE
                moved = shifted(run, (target - start) % 128)
                tile, first = divmod(target, 128)
                if tile < 2:
                    put(main, tile, first, moved)
                    if tile == 0 and first + WIDE > 128:
                        put(main, 1, 0, moved)
                beyond = max(target - 256, 0)
                if target + WIDE > 256 and group < 2:
                    put(tail, group, beyond, moved)
                elif target + WIDE > 256:
                    if beyond < SPARE:
                        put(tail, 0, TAIL + beyond, shifted(run, (target - start + TAIL) % 128))
                    if target + WIDE - 256 > SPARE:
                        put(tail, 1, TAIL + max(beyond - SPARE, 0), shifted(run, (target - start + TAIL - SPARE) % 128))
            block[dest, rows, :] = main[0]
            block[dest, OWN_IFGS + GROUP * group : OWN_IFGS + GROUP * (group + 1), :] = main[1]
        block[dest, 2 * OWN_IFGS : 2 * OWN_IFGS + GROUP, :] = tail[0]
        block[dest, 2 * OWN_IFGS + GROUP :, :] = tail[1]

    stores = []
    for chunk in range(CHUNKS):
        for load in loads[chunk]:
            load.wait()
        for row in range(ROWS):
            first = CHUNK * chunk
            values = phase[row, :, first : first + CHUNK] * mask[row, :, first : first + CHUNK].astype(jnp.float32)
            masked[row, :, 128 + first : 128 + first + CHUNK] = values
        for dest in range(IFG_COUNT):
            if needed_chunk(dest) == chunk:
                fill(dest)
                if (dest + 1) % STORE == 0:
                    at = pl.ds(dest + 1 - STORE, STORE)
                    store = pltpu.make_async_copy(block.at[at], out_ref.at[at], out_sem.at[dest // STORE])
                    store.start()
                    stores.append(store)
    for store in stores:
        store.wait()


def pack(unwrapped, component_mask):
    anywhere = pl.BlockSpec(memory_space=pl.ANY)
    columns = CHUNKS * CHUNK
    return pl.pallas_call(
        pack_kernel,
        in_specs=[anywhere] * 2,
        out_specs=anywhere,
        out_shape=jax.ShapeDtypeStruct((IFG_COUNT, BLOCK, 128), jnp.float32),
        scratch_shapes=[
            pltpu.VMEM((ROWS, OWN_IFGS, columns), jnp.float32),
            pltpu.VMEM((ROWS, OWN_IFGS, columns), jnp.int32),
            pltpu.VMEM((ROWS, OWN_IFGS, columns + 256), jnp.float32),
            pltpu.VMEM((IFG_COUNT, BLOCK, 128), jnp.float32),
            pltpu.SemaphoreType.DMA((2, CHUNKS)),
            pltpu.SemaphoreType.DMA((IFG_COUNT // STORE,)),
        ],
        compiler_params=pltpu.CompilerParams(vmem_limit_bytes=56 * MIB),
        cost_estimate=pl.CostEstimate(flops=2_000_000, bytes_accessed=5_600_000, transcendentals=0),
        name="mask_pack",
    )(unwrapped, component_mask)


def iota(shape, dim):
    return lax.broadcasted_iota(jnp.int32, shape, dim)


def one_hot(pairs, dates):
    date = iota((dates, pairs.shape[1]), 0)
    later = jnp.where(pairs[1:2, :] == date, 1.0, 0.0)
    return (later - jnp.where(pairs[0:1, :] == date, 1.0, 0.0)).astype(jnp.bfloat16)


def identity(rows, cols, first=0):
    return jnp.where(iota((rows, cols), 0) + first == iota((rows, cols), 1), 1.0, 0.0)


def eliminate(normal_ref, band_ref, lower_ref, scaled_ref):
    window = SPAN // 8 + 1
    blocks = DATE_ROWS // 8
    for tile in range(window, window + blocks):
        start = 8 * tile - SPAN
        rows = normal_ref[8 * tile : 8 * tile + 8, :]
        band_ref[8 * tile : 8 * tile + 8, :] = pltpu.roll(rows, (DATE_LANES - start) % DATE_LANES, 1)[:, :128]
    sub = iota((8, 128), 0)
    lane = iota((8, 128), 1)

    def block_step(block, carry):
        left, right = list(carry[:window]), list(carry[window:])
        pivots = jnp.zeros((8, 128), jnp.float32)
        for j in range(8):
            pivot_row = left[0][j : j + 1, :]
            right_row = right[0][j : j + 1, :]
            scale = jnp.broadcast_to(1.0 / pivot_row[:, j : j + 1], (8, 128))
            pivots = jnp.where(sub == j, scale, pivots)
            scaled_row = pivot_row * scale[0:1, :]
            scaled_right = right_row * jnp.concatenate([scale[0:1, :]] * 3, axis=1)
            for q in range(window):
                factor = jnp.broadcast_to(left[q][:, j : j + 1], (8, 128))
                if q == 0:
                    factor = jnp.where(sub > j, factor, 0.0)
                left[q] = left[q] - factor * scaled_row
                right[q] = right[q] - jnp.concatenate([factor] * 3, axis=1) * scaled_right
        at = pl.ds(pl.multiple_of(8 * block, 8), 8)
        lower_ref[at, :] = right[0]
        scaled_ref[at, :] = right[0] * jnp.concatenate([pivots] * 3, axis=1)
        entering = pl.multiple_of(8 * (block + window), 8)
        left = [jnp.where(lane < 120, pltpu.roll(part, 120, 1), 0.0) for part in left[1:]]
        left.append(band_ref[pl.ds(entering, 8), :])
        right = right[1:] + [identity(8, DATE_LANES, entering)]
        return tuple(left + right)

    left = [normal_ref[8 * q : 8 * q + 8, 0:128] for q in range(window)]
    right = [identity(8, DATE_LANES, 8 * q) for q in range(window)]
    lax.fori_loop(0, blocks, block_step, tuple(left + right))


def highpass_matrix():
    row, col = iota((DATE_ROWS, DATE_LANES), 0), iota((DATE_ROWS, DATE_LANES), 1)
    spread = (row - col).astype(jnp.float32)
    weights = jnp.exp(-spread * spread / (2.0 * TIME_SIGMA * TIME_SIGMA))
    weights = jnp.where(col < DATES, weights, 0.0)
    lowpass = weights / jnp.sum(weights, axis=1, keepdims=True)
    return jnp.where((row < DATES) & (col < DATES), identity(DATE_ROWS, DATE_LANES) - lowpass, 0.0)


def tap(offset):
    sigma = RIM_WIDTH / 2.0
    return jnp.where(jnp.abs(offset) <= RIM_WIDTH, jnp.exp(-offset * offset / (2.0 * sigma * sigma)), 0.0)


def split_three(value):
    first = value.astype(jnp.bfloat16)
    rest = value - first.astype(jnp.float32)
    second = rest.astype(jnp.bfloat16)
    return first, second, (rest - second.astype(jnp.float32)).astype(jnp.bfloat16)


def operators_kernel(pairs_ref, solve_ref, first_ref, second_ref, third_ref, normal_ref, band_ref, lower_ref, scaled_ref):
    design = one_hot(pairs_ref[...], DATE_LANES)
    normal = lax.dot_general(design, design, (((1,), (1,)), ((), ())), preferred_element_type=jnp.float32)
    normal_ref[...] = normal + identity(DATE_LANES, DATE_LANES)
    eliminate(normal_ref, band_ref, lower_ref, scaled_ref)
    solve = lax.dot_general(lower_ref[...], scaled_ref[...], (((0,), (0,)), ((), ())),
                            precision=lax.Precision.HIGHEST, preferred_element_type=jnp.float32)
    solve_ref[...] = solve[:DATE_ROWS]
    first_ref[...], second_ref[...], third_ref[...] = split_three(full_dot(highpass_matrix(), solve))


def operators(pairs):
    part = jax.ShapeDtypeStruct((DATE_ROWS, DATE_LANES), jnp.bfloat16)
    return pl.pallas_call(
        operators_kernel,
        in_specs=[WHOLE],
        out_specs=[WHOLE] * 4,
        out_shape=[jax.ShapeDtypeStruct((DATE_ROWS, DATE_LANES), jnp.float32)] + [part] * 3,
        scratch_shapes=[
            pltpu.VMEM((DATE_LANES, DATE_LANES), jnp.float32),
            pltpu.VMEM((DATE_LANES, 128), jnp.float32),
            pltpu.VMEM((DATE_ROWS, DATE_LANES), jnp.float32),
            pltpu.VMEM((DATE_ROWS, DATE_LANES), jnp.float32),
        ],
        compiler_params=pltpu.CompilerParams(vmem_limit_bytes=24 * MIB),
        cost_estimate=pl.CostEstimate(flops=20_000_000_000, bytes_accessed=3_000_000, transcendentals=0),
        name="operators",
    )(pairs)


def padded(value):
    return jnp.concatenate([value, jnp.zeros((DATE_LANES - DATE_ROWS, LANES), jnp.float32)], axis=0)


def gather_dates(ordered_ref, data_ref):
    def block(start):
        return split(data_ref[:, start : start + GROUP, :].reshape(GROUP * IFG_COUNT, 128))

    tails = [block(2 * OWN_IFGS), block(2 * OWN_IFGS + GROUP)]
    main, rest, spare = None, None, None
    for group in range(GROUPS):
        parts = [block(GROUP * group), block(OWN_IFGS + GROUP * group)]
        parts += tails if group == 2 else [tails[group]]
        design = one_hot(ordered_ref[:, 512 * group : 512 * group + 512], DATE_ROWS)
        high = jnp.concatenate([part[0] for part in parts], axis=1)
        low = jnp.concatenate([part[1] for part in parts], axis=1)
        sums = dot(design, high) + dot(design, low)
        main = sums[:, :256] if main is None else main + sums[:, :256]
        if group == 2:
            spare = sums[:, 256:]
        else:
            rest = sums[:, 256:] if rest is None else rest + sums[:, 256:]
    lane = iota((DATE_ROWS, 128), 1)
    first, second = shifted(spare[:, :128], 128 - TAIL), shifted(spare[:, 128:], 128 - TAIL + SPARE)
    rest = jnp.where(lane < TAIL, rest + jnp.where(lane < SPARE, first, second), 0.0)
    return jnp.concatenate([main, rest], axis=1)


def weight(offset):
    sigma = RIM_WIDTH / 2.0
    return float(np.exp(-offset * offset / (2.0 * sigma * sigma)))


def send_edge(edge_ref, own_ref, first):
    half = RIM_WIDTH // 2
    lane = iota((COLS, 128), 1)

    def own(place, tile):
        start = COLS * (first + place)
        return own_ref[start : start + COLS, 128 * tile : 128 * (tile + 1)]

    for place in range(RIM_WIDTH):
        for tile in range(2):
            start = EDGE_PIXELS * tile + COLS * place
            edge_ref[start : start + COLS, :] = own(place, tile)
    for place in range(half):
        start = 2 * EDGE_PIXELS + COLS * place
        edge_ref[start : start + COLS, :] = jnp.where(lane < 64, own(place, 2), pltpu.roll(own(place + half, 2), 64, 1))


def varying_kernel(ordered_ref, data_ref, first_ref, second_ref, third_ref, scale_ref, sums_ref, own_ref,
                   edge_a_ref, edge_b_ref, wide_ref):
    sums = padded(gather_dates(ordered_ref, data_ref))
    sums_ref[...] = sums
    left = [first_ref[...], second_ref[...], third_ref[...]]
    right = split_three(sums)
    orders = ((2, 0), (0, 2), (1, 1), (1, 0), (0, 1), (0, 0))
    varying = dot(
        jnp.concatenate([left[i] for i, _ in orders], axis=1), jnp.concatenate([right[j] for _, j in orders], axis=0)
    )
    varying = padded(varying).T
    for tile in range(3):
        wide_ref[tile] = varying[:, 128 * tile : 128 * (tile + 1)]
        for row in range(ROWS):
            start = WIDE * row + RIM_WIDTH
            total = wide_ref[tile, start : start + COLS, :]
            for offset in range(1, RIM_WIDTH + 1):
                both = wide_ref[tile, start - offset : start - offset + COLS, :]
                both = both + wide_ref[tile, start + offset : start + offset + COLS, :]
                total = total + weight(offset) * both
            own_ref[COLS * row : COLS * (row + 1), 128 * tile : 128 * (tile + 1)] = total * scale_ref[...]
    for core, (edge_down, edge_up) in enumerate(((edge_a_ref, edge_b_ref), (edge_b_ref, edge_a_ref))):

        @pl.when(lax.axis_index("ifg") % 2 == core)
        def _():
            send_edge(edge_down, own_ref, ROWS - RIM_WIDTH)
            send_edge(edge_up, own_ref, 0)


def project_varying(ordered, data, filtered, column_scale):
    edge = jax.ShapeDtypeStruct((EDGE_ROWS, 128), jnp.float32)
    return pl.pallas_call(
        varying_kernel,
        in_specs=[WHOLE] * 6,
        out_specs=[WHOLE] * 4,
        out_shape=[
            jax.ShapeDtypeStruct((DATE_LANES, LANES), jnp.float32),
            jax.ShapeDtypeStruct((PIXELS, DATE_LANES), jnp.float32),
            edge,
            edge,
        ],
        scratch_shapes=[pltpu.VMEM((3, LANES, 128), jnp.float32)],
        compiler_params=pltpu.CompilerParams(vmem_limit_bytes=24 * MIB),
        cost_estimate=pl.CostEstimate(flops=1_100_000_000, bytes_accessed=5_000_000, transcendentals=0),
        name="varying",
    )(ordered, data, *filtered, column_scale)


def series_kernel(scale_ref, solve_ref, sums_ref, smooth_ref, series_ref, partial_ref):
    series = padded(full_dot(solve_ref[...], sums_ref[...])).T
    for row in range(ROWS):
        start = WIDE * row + RIM_WIDTH
        own = series[start : start + COLS]
        series_ref[row] = own[:, :DATES]
        total = None
        for other in range(ROWS):
            if abs(other - row) <= RIM_WIDTH:
                term = weight(other - row) * smooth_ref[COLS * other : COLS * (other + 1), :]
                total = term if total is None else total + term
        partial_ref[COLS * row : COLS * (row + 1), :] = own - total * jnp.concatenate([scale_ref[row : row + 1, :]] * 3, axis=1)


def project_series(row_scale, solve, sums, smooth):
    return pl.pallas_call(
        series_kernel,
        in_specs=[WHOLE] * 4,
        out_specs=[WHOLE] * 2,
        out_shape=[
            jax.ShapeDtypeStruct((ROWS, COLS, DATES), jnp.float32),
            jax.ShapeDtypeStruct((PIXELS, DATE_LANES), jnp.float32),
        ],
        compiler_params=pltpu.CompilerParams(vmem_limit_bytes=16 * MIB),
        cost_estimate=pl.CostEstimate(flops=2_000_000_000, bytes_accessed=2_000_000, transcendentals=0),
        name="series",
    )(row_scale, solve, sums, smooth)


def edge_tile(edge_ref, row, tile):
    if tile < 2:
        start = EDGE_PIXELS * tile + COLS * row
        return edge_ref[start : start + COLS, :]
    start = 2 * EDGE_PIXELS + COLS * (row % 2)
    return shifted(edge_ref[start : start + COLS, :], 64 * (row // 2))


def corrected_kernel(scale_ref, partial_ref, edge_a_ref, edge_b_ref, out_ref):
    for core, (above_ref, below_ref) in enumerate(((edge_a_ref, edge_b_ref), (edge_b_ref, edge_a_ref))):

        @pl.when(lax.axis_index("ifg") % 2 == core)
        def _():
            for row in range(ROWS):
                near = [(other - RIM_WIDTH - row, above_ref, other) for other in range(RIM_WIDTH)]
                near += [(ROWS + other - row, below_ref, other) for other in range(RIM_WIDTH)]
                near = [entry for entry in near if abs(entry[0]) <= RIM_WIDTH]
                scale = scale_ref[row : row + 1, :]
                for tile in range(3):
                    total = sum(weight(offset) * edge_tile(ref, other, tile) for offset, ref, other in near)
                    part = partial_ref[COLS * row : COLS * (row + 1), 128 * tile : 128 * (tile + 1)]
                    width = min(128, DATES - 128 * tile)
                    out_ref[row, :, 128 * tile : 128 * tile + width] = (part - total * scale)[:, :width]


def correct(row_scale, partial, edge_a, edge_b):
    return pl.pallas_call(
        corrected_kernel,
        in_specs=[WHOLE] * 4,
        out_specs=WHOLE,
        out_shape=jax.ShapeDtypeStruct((ROWS, COLS, DATES), jnp.float32),
        compiler_params=pltpu.CompilerParams(vmem_limit_bytes=16 * MIB),
        cost_estimate=pl.CostEstimate(flops=1_000_000, bytes_accessed=1_400_000, transcendentals=0),
        name="corrected",
    )(row_scale, partial, edge_a, edge_b)


def pass_on(edge, first_way):
    pairs = []
    for i in range(IFG_COUNT):
        way = first_way if i % 2 == 0 else -first_way
        for b in range(BAND_COUNT):
            if 0 <= b + way < BAND_COUNT:
                pairs.append((i * BAND_COUNT + b, i * BAND_COUNT + b + way))
    return lax.ppermute(edge, ("ifg", "band"), pairs)


def edge_weights(start, count, total):
    offsets = jnp.arange(-RIM_WIDTH, RIM_WIDTH + 1, dtype=jnp.int32)
    places = start + jnp.arange(count, dtype=jnp.int32)[:, None] + offsets[None, :]
    inside = ((places >= 0) & (places < total)).astype(jnp.float32)
    return jnp.sum(inside * tap(offsets.astype(jnp.float32))[None, :], axis=1)


def body(unwrapped, component_mask, date_pairs):
    blocks = pack(unwrapped.transpose(1, 0, 2), component_mask.transpose(1, 0, 2))
    data = lax.all_to_all(blocks, "ifg", split_axis=0, concat_axis=0, tiled=True)
    row_norm = edge_weights(lax.axis_index("band") * ROWS, ROWS, ROWS * BAND_COUNT)
    row_scale = jnp.broadcast_to((1.0 / row_norm)[:, None], (ROWS, 128))
    column_norm = edge_weights(lax.axis_index("ifg") * COLS, COLS, COLS * IFG_COUNT)
    pairs = date_pairs.T
    ordered = pairs.reshape(2, IFG_COUNT, GROUPS, GROUP).transpose(0, 2, 1, 3).reshape(2, IFGS)
    column_scale = jnp.broadcast_to((1.0 / column_norm)[:, None], (COLS, 128))
    solve, *filtered = operators(pairs)
    sums, smooth, edge_a, edge_b = project_varying(ordered, data, filtered, column_scale)
    edge_a, edge_b = pass_on(edge_a, 1), pass_on(edge_b, -1)
    series, partial = project_series(row_scale, solve, sums, smooth)
    corrected = correct(row_scale, partial, edge_a, edge_b)
    return series.transpose(2, 0, 1), corrected.transpose(2, 0, 1)


def solution(mesh):
    placed = (P("ifg", "band", None), P("ifg", "band", None), P())
    return jax.shard_map(
        body,
        mesh=mesh,
        in_specs=placed,
        out_specs=(P(None, "band", "ifg"), P(None, "band", "ifg")),
        check_vma=False,
    )
```

```python
import jax
import jax.numpy as jnp
import numpy as np
from jax import lax
from jax.experimental import pallas as pl
from jax.experimental.pallas import tpu as pltpu
from jax.sharding import PartitionSpec as P

DATES = 300
SPAN = 40
TIME_SIGMA = 6
RIM_WIDTH = 4

DATE_ROWS = 304
DATE_LANES = 384

IFG_COUNT = 32
BAND_COUNT = 16
OWN_IFGS = 48
ROWS = 6
COLS = 48
PIXELS = ROWS * COLS
IFGS = IFG_COUNT * OWN_IFGS

WIDE = COLS + 2 * RIM_WIDTH
WIDE_PIXELS = ROWS * WIDE
LANES = 384

GROUP = 16
GROUPS = OWN_IFGS // GROUP
TAIL = WIDE_PIXELS - 256
SPARE = 128 - TAIL
BLOCK = 2 * OWN_IFGS + 2 * GROUP
CHUNKS = 4
CHUNK = IFG_COUNT * COLS // CHUNKS
STORE = 4

EDGE_PIXELS = RIM_WIDTH * COLS
EDGE_ROWS = 2 * EDGE_PIXELS + EDGE_PIXELS // 2
MIB = 1024 * 1024
WHOLE = pl.BlockSpec(memory_space=pltpu.VMEM)


def split(value):
    high = value.astype(jnp.bfloat16)
    low = (value - high.astype(jnp.float32)).astype(jnp.bfloat16)
    return high, low


def dot(a, b):
    return jnp.dot(a, b, preferred_element_type=jnp.float32)


def full_dot(a, b):
    return jnp.dot(a, b, precision=lax.Precision.HIGHEST, preferred_element_type=jnp.float32)


def shifted(value, shift):
    return value if shift == 0 else pltpu.roll(value, shift, 1)


def needed_chunk(dest):
    last = dest * COLS + COLS + RIM_WIDTH - 1
    return min(last, IFG_COUNT * COLS - 1) // CHUNK


def pack_kernel(unwrapped_ref, mask_ref, out_ref, phase, mask, masked, block, in_sem, out_sem):
    loads = []
    for chunk in range(CHUNKS):
        at = (slice(None), slice(None), pl.ds(CHUNK * chunk, CHUNK))
        pair = (
            pltpu.make_async_copy(unwrapped_ref.at[at], phase.at[at], in_sem.at[0, chunk]),
            pltpu.make_async_copy(mask_ref.at[at], mask.at[at], in_sem.at[1, chunk]),
        )
        for load in pair:
            load.start()
        loads.append(pair)
    width = CHUNKS * CHUNK
    for row in range(ROWS):
        masked[row, :, 0:128] = jnp.zeros((OWN_IFGS, 128), jnp.float32)
        masked[row, :, 128 + width : 256 + width] = jnp.zeros((OWN_IFGS, 128), jnp.float32)
    lane = lax.broadcasted_iota(jnp.int32, (GROUP, 128), 1)

    def fill(dest):
        source_tile, start = divmod(128 + dest * COLS - RIM_WIDTH, 128)
        tail = [None] * 2
        for group in range(GROUPS):
            rows = slice(GROUP * group, GROUP * (group + 1))
            main = [None] * 2

            def put(parts, tile, first, moved):
                parts[tile] = moved if first == 0 else jnp.where(lane >= first, moved, parts[tile])

            for row in range(ROWS):
                run = masked[row, rows, 128 * source_tile : 128 * source_tile + 128]
                if start + WIDE > 128:
                    rest = masked[row, rows, 128 * source_tile + 128 : 128 * source_tile + 256]
                    run = jnp.where(lane >= start, run, rest)
                target = row * WIDE
                moved = shifted(run, (target - start) % 128)
                tile, first = divmod(target, 128)
                if tile < 2:
                    put(main, tile, first, moved)
                    if tile == 0 and first + WIDE > 128:
                        put(main, 1, 0, moved)
                beyond = max(target - 256, 0)
                if target + WIDE > 256 and group < 2:
                    put(tail, group, beyond, moved)
                elif target + WIDE > 256:
                    if beyond < SPARE:
                        put(tail, 0, TAIL + beyond, shifted(run, (target - start + TAIL) % 128))
                    if target + WIDE - 256 > SPARE:
                        put(tail, 1, TAIL + max(beyond - SPARE, 0), shifted(run, (target - start + TAIL - SPARE) % 128))
            block[dest, rows, :] = main[0]
            block[dest, OWN_IFGS + GROUP * group : OWN_IFGS + GROUP * (group + 1), :] = main[1]
        block[dest, 2 * OWN_IFGS : 2 * OWN_IFGS + GROUP, :] = tail[0]
        block[dest, 2 * OWN_IFGS + GROUP :, :] = tail[1]

    stores = []
    for chunk in range(CHUNKS):
        for load in loads[chunk]:
            load.wait()
        for row in range(ROWS):
            first = CHUNK * chunk
            inside = mask[row, :, first : first + CHUNK] != 0
            values = jnp.where(inside, phase[row, :, first : first + CHUNK], 0.0)
            masked[row, :, 128 + first : 128 + first + CHUNK] = values
        for dest in range(IFG_COUNT):
            if needed_chunk(dest) == chunk:
                fill(dest)
                if (dest + 1) % STORE == 0:
                    at = pl.ds(dest + 1 - STORE, STORE)
                    store = pltpu.make_async_copy(block.at[at], out_ref.at[at], out_sem.at[dest // STORE])
                    store.start()
                    stores.append(store)
    for store in stores:
        store.wait()


def pack(unwrapped, component_mask):
    anywhere = pl.BlockSpec(memory_space=pl.ANY)
    columns = CHUNKS * CHUNK
    return pl.pallas_call(
        pack_kernel,
        in_specs=[anywhere] * 2,
        out_specs=anywhere,
        out_shape=jax.ShapeDtypeStruct((IFG_COUNT, BLOCK, 128), jnp.float32),
        scratch_shapes=[
            pltpu.VMEM((ROWS, OWN_IFGS, columns), jnp.float32),
            pltpu.VMEM((ROWS, OWN_IFGS, columns), jnp.int32),
            pltpu.VMEM((ROWS, OWN_IFGS, columns + 256), jnp.float32),
            pltpu.VMEM((IFG_COUNT, BLOCK, 128), jnp.float32),
            pltpu.SemaphoreType.DMA((2, CHUNKS)),
            pltpu.SemaphoreType.DMA((IFG_COUNT // STORE,)),
        ],
        compiler_params=pltpu.CompilerParams(vmem_limit_bytes=56 * MIB),
        cost_estimate=pl.CostEstimate(flops=2_000_000, bytes_accessed=5_600_000, transcendentals=0),
        name="mask_pack",
    )(unwrapped, component_mask)


def iota(shape, dim):
    return lax.broadcasted_iota(jnp.int32, shape, dim)


def one_hot(pairs, dates):
    date = iota((dates, pairs.shape[1]), 0)
    earlier = jnp.where(pairs[0:1, :] == date, -1.0, 0.0)
    return jnp.where(pairs[1:2, :] == date, 1.0, earlier).astype(jnp.bfloat16)


def identity(rows, cols, first=0):
    return jnp.where(iota((rows, cols), 0) + first == iota((rows, cols), 1), 1.0, 0.0)


def eliminate(normal_ref, band_ref, lower_ref, scaled_ref):
    window = SPAN // 8 + 1
    blocks = DATE_ROWS // 8
    for tile in range(window, window + blocks):
        start = 8 * tile - SPAN
        rows = normal_ref[8 * tile : 8 * tile + 8, :]
        band_ref[8 * tile : 8 * tile + 8, :] = pltpu.roll(rows, (DATE_LANES - start) % DATE_LANES, 1)[:, :128]
    sub = iota((8, 128), 0)
    lane = iota((8, 128), 1)

    def block_step(block, carry):
        left, right = list(carry[:window]), list(carry[window:])
        pivots = jnp.zeros((8, 128), jnp.float32)
        for j in range(8):
            pivot_row = left[0][j : j + 1, :]
            right_row = right[0][j : j + 1, :]
            scale = jnp.broadcast_to(1.0 / pivot_row[:, j : j + 1], (8, 128))
            pivots = jnp.where(sub == j, scale, pivots)
            scaled_row = pivot_row * scale[0:1, :]
            scaled_right = right_row * jnp.concatenate([scale[0:1, :]] * 3, axis=1)
            for q in range(window):
                factor = jnp.broadcast_to(left[q][:, j : j + 1], (8, 128))
                if q == 0:
                    factor = jnp.where(sub > j, factor, 0.0)
                left[q] = left[q] - factor * scaled_row
                right[q] = right[q] - jnp.concatenate([factor] * 3, axis=1) * scaled_right
        at = pl.ds(pl.multiple_of(8 * block, 8), 8)
        lower_ref[at, :] = right[0]
        scaled_ref[at, :] = right[0] * jnp.concatenate([pivots] * 3, axis=1)
        entering = pl.multiple_of(8 * (block + window), 8)
        left = [jnp.where(lane < 120, pltpu.roll(part, 120, 1), 0.0) for part in left[1:]]
        left.append(band_ref[pl.ds(entering, 8), :])
        right = right[1:] + [identity(8, DATE_LANES, entering)]
        return tuple(left + right)

    left = [normal_ref[8 * q : 8 * q + 8, 0:128] for q in range(window)]
    right = [identity(8, DATE_LANES, 8 * q) for q in range(window)]
    lax.fori_loop(0, blocks, block_step, tuple(left + right))


def highpass_matrix():
    row, col = iota((DATE_ROWS, DATE_LANES), 0), iota((DATE_ROWS, DATE_LANES), 1)
    spread = (row - col).astype(jnp.float32)
    weights = jnp.exp(-spread * spread / (2.0 * TIME_SIGMA * TIME_SIGMA))
    weights = jnp.where(col < DATES, weights, 0.0)
    lowpass = weights / jnp.sum(weights, axis=1, keepdims=True)
    return jnp.where((row < DATES) & (col < DATES), identity(DATE_ROWS, DATE_LANES) - lowpass, 0.0)


def tap(offset):
    sigma = RIM_WIDTH / 2.0
    return jnp.where(jnp.abs(offset) <= RIM_WIDTH, jnp.exp(-offset * offset / (2.0 * sigma * sigma)), 0.0)


def split_three(value):
    first = value.astype(jnp.bfloat16)
    rest = value - first.astype(jnp.float32)
    second = rest.astype(jnp.bfloat16)
    return first, second, (rest - second.astype(jnp.float32)).astype(jnp.bfloat16)


def operators_kernel(pairs_ref, solve_ref, first_ref, second_ref, third_ref, normal_ref, band_ref, lower_ref, scaled_ref):
    design = one_hot(pairs_ref[...], DATE_LANES)
    normal = lax.dot_general(design, design, (((1,), (1,)), ((), ())), preferred_element_type=jnp.float32)
    normal_ref[...] = normal + identity(DATE_LANES, DATE_LANES)
    eliminate(normal_ref, band_ref, lower_ref, scaled_ref)
    solve = lax.dot_general(lower_ref[...], scaled_ref[...], (((0,), (0,)), ((), ())),
                            precision=lax.Precision.HIGHEST, preferred_element_type=jnp.float32)
    solve_ref[...] = solve[:DATE_ROWS]
    first_ref[...], second_ref[...], third_ref[...] = split_three(full_dot(highpass_matrix(), solve))


def operators(pairs):
    part = jax.ShapeDtypeStruct((DATE_ROWS, DATE_LANES), jnp.bfloat16)
    return pl.pallas_call(
        operators_kernel,
        in_specs=[WHOLE],
        out_specs=[WHOLE] * 4,
        out_shape=[jax.ShapeDtypeStruct((DATE_ROWS, DATE_LANES), jnp.float32)] + [part] * 3,
        scratch_shapes=[
            pltpu.VMEM((DATE_LANES, DATE_LANES), jnp.float32),
            pltpu.VMEM((DATE_LANES, 128), jnp.float32),
            pltpu.VMEM((DATE_ROWS, DATE_LANES), jnp.float32),
            pltpu.VMEM((DATE_ROWS, DATE_LANES), jnp.float32),
        ],
        compiler_params=pltpu.CompilerParams(vmem_limit_bytes=24 * MIB),
        cost_estimate=pl.CostEstimate(flops=20_000_000_000, bytes_accessed=3_000_000, transcendentals=0),
        name="operators",
    )(pairs)


def padded(value):
    return jnp.concatenate([value, jnp.zeros((DATE_LANES - DATE_ROWS, LANES), jnp.float32)], axis=0)


def gather_dates(ordered_ref, data_ref):
    def block(start):
        return split(data_ref[:, start : start + GROUP, :].reshape(GROUP * IFG_COUNT, 128))

    tails = [block(2 * OWN_IFGS), block(2 * OWN_IFGS + GROUP)]
    main, rest, spare = None, None, None
    for group in range(GROUPS):
        parts = [block(GROUP * group), block(OWN_IFGS + GROUP * group)]
        parts += tails if group == 2 else [tails[group]]
        design = one_hot(ordered_ref[:, 512 * group : 512 * group + 512], DATE_ROWS)
        high = jnp.concatenate([part[0] for part in parts], axis=1)
        low = jnp.concatenate([part[1] for part in parts], axis=1)
        sums = dot(design, high) + dot(design, low)
        main = sums[:, :256] if main is None else main + sums[:, :256]
        if group == 2:
            spare = sums[:, 256:]
        else:
            rest = sums[:, 256:] if rest is None else rest + sums[:, 256:]
    lane = iota((DATE_ROWS, 128), 1)
    first, second = shifted(spare[:, :128], 128 - TAIL), shifted(spare[:, 128:], 128 - TAIL + SPARE)
    rest = jnp.where(lane < TAIL, rest + jnp.where(lane < SPARE, first, second), 0.0)
    return jnp.concatenate([main, rest], axis=1)


def weight(offset):
    sigma = RIM_WIDTH / 2.0
    return float(np.exp(-offset * offset / (2.0 * sigma * sigma)))


def send_edge(edge_ref, own_ref, first):
    half = RIM_WIDTH // 2
    lane = iota((COLS, 128), 1)

    def own(place, tile):
        start = COLS * (first + place)
        return own_ref[start : start + COLS, 128 * tile : 128 * (tile + 1)]

    for place in range(RIM_WIDTH):
        for tile in range(2):
            start = EDGE_PIXELS * tile + COLS * place
            edge_ref[start : start + COLS, :] = own(place, tile)
    for place in range(half):
        start = 2 * EDGE_PIXELS + COLS * place
        edge_ref[start : start + COLS, :] = jnp.where(lane < 64, own(place, 2), pltpu.roll(own(place + half, 2), 64, 1))


def varying_kernel(ordered_ref, data_ref, first_ref, second_ref, third_ref, scale_ref, sums_ref, own_ref,
                   edge_a_ref, edge_b_ref, wide_ref):
    sums = padded(gather_dates(ordered_ref, data_ref))
    sums_ref[...] = sums
    left = [first_ref[...], second_ref[...], third_ref[...]]
    right = split_three(sums)
    orders = ((2, 0), (0, 2), (1, 1), (1, 0), (0, 1), (0, 0))
    varying = dot(
        jnp.concatenate([left[i] for i, _ in orders], axis=1), jnp.concatenate([right[j] for _, j in orders], axis=0)
    )
    varying = padded(varying).T
    for tile in range(3):
        wide_ref[tile] = varying[:, 128 * tile : 128 * (tile + 1)]
        for row in range(ROWS):
            start = WIDE * row + RIM_WIDTH
            total = wide_ref[tile, start : start + COLS, :]
            for offset in range(1, RIM_WIDTH + 1):
                both = wide_ref[tile, start - offset : start - offset + COLS, :]
                both = both + wide_ref[tile, start + offset : start + offset + COLS, :]
                total = total + weight(offset) * both
            own_ref[COLS * row : COLS * (row + 1), 128 * tile : 128 * (tile + 1)] = total * scale_ref[...]
    for core, (edge_down, edge_up) in enumerate(((edge_a_ref, edge_b_ref), (edge_b_ref, edge_a_ref))):

        @pl.when(lax.axis_index("ifg") % 2 == core)
        def _():
            send_edge(edge_down, own_ref, ROWS - RIM_WIDTH)
            send_edge(edge_up, own_ref, 0)


def project_varying(ordered, data, filtered, column_scale):
    edge = jax.ShapeDtypeStruct((EDGE_ROWS, 128), jnp.float32)
    return pl.pallas_call(
        varying_kernel,
        in_specs=[WHOLE] * 6,
        out_specs=[WHOLE] * 4,
        out_shape=[
            jax.ShapeDtypeStruct((DATE_LANES, LANES), jnp.float32),
            jax.ShapeDtypeStruct((PIXELS, DATE_LANES), jnp.float32),
            edge,
            edge,
        ],
        scratch_shapes=[pltpu.VMEM((3, LANES, 128), jnp.float32)],
        compiler_params=pltpu.CompilerParams(vmem_limit_bytes=24 * MIB),
        cost_estimate=pl.CostEstimate(flops=1_100_000_000, bytes_accessed=5_000_000, transcendentals=0),
        name="varying",
    )(ordered, data, *filtered, column_scale)


def series_kernel(scale_ref, solve_ref, sums_ref, smooth_ref, series_ref, partial_ref):
    series = padded(full_dot(solve_ref[...], sums_ref[...])).T
    for row in range(ROWS):
        start = WIDE * row + RIM_WIDTH
        own = series[start : start + COLS]
        series_ref[row] = own[:, :DATES]
        total = None
        for other in range(ROWS):
            if abs(other - row) <= RIM_WIDTH:
                term = weight(other - row) * smooth_ref[COLS * other : COLS * (other + 1), :]
                total = term if total is None else total + term
        partial_ref[COLS * row : COLS * (row + 1), :] = own - total * jnp.concatenate([scale_ref[row : row + 1, :]] * 3, axis=1)


def project_series(row_scale, solve, sums, smooth):
    return pl.pallas_call(
        series_kernel,
        in_specs=[WHOLE] * 4,
        out_specs=[WHOLE] * 2,
        out_shape=[
            jax.ShapeDtypeStruct((ROWS, COLS, DATES), jnp.float32),
            jax.ShapeDtypeStruct((PIXELS, DATE_LANES), jnp.float32),
        ],
        compiler_params=pltpu.CompilerParams(vmem_limit_bytes=16 * MIB),
        cost_estimate=pl.CostEstimate(flops=2_000_000_000, bytes_accessed=2_000_000, transcendentals=0),
        name="series",
    )(row_scale, solve, sums, smooth)


def edge_tile(edge_ref, row, tile):
    if tile < 2:
        start = EDGE_PIXELS * tile + COLS * row
        return edge_ref[start : start + COLS, :]
    start = 2 * EDGE_PIXELS + COLS * (row % 2)
    return shifted(edge_ref[start : start + COLS, :], 64 * (row // 2))


def corrected_kernel(scale_ref, partial_ref, edge_a_ref, edge_b_ref, out_ref):
    for core, (above_ref, below_ref) in enumerate(((edge_a_ref, edge_b_ref), (edge_b_ref, edge_a_ref))):

        @pl.when(lax.axis_index("ifg") % 2 == core)
        def _():
            for row in range(ROWS):
                near = [(other - RIM_WIDTH - row, above_ref, other) for other in range(RIM_WIDTH)]
                near += [(ROWS + other - row, below_ref, other) for other in range(RIM_WIDTH)]
                near = [entry for entry in near if abs(entry[0]) <= RIM_WIDTH]
                scale = scale_ref[row : row + 1, :]
                for tile in range(3):
                    total = sum(weight(offset) * edge_tile(ref, other, tile) for offset, ref, other in near)
                    part = partial_ref[COLS * row : COLS * (row + 1), 128 * tile : 128 * (tile + 1)]
                    width = min(128, DATES - 128 * tile)
                    out_ref[row, :, 128 * tile : 128 * tile + width] = (part - total * scale)[:, :width]


def correct(row_scale, partial, edge_a, edge_b):
    return pl.pallas_call(
        corrected_kernel,
        in_specs=[WHOLE] * 4,
        out_specs=WHOLE,
        out_shape=jax.ShapeDtypeStruct((ROWS, COLS, DATES), jnp.float32),
        compiler_params=pltpu.CompilerParams(vmem_limit_bytes=16 * MIB),
        cost_estimate=pl.CostEstimate(flops=1_000_000, bytes_accessed=1_400_000, transcendentals=0),
        name="corrected",
    )(row_scale, partial, edge_a, edge_b)


def pass_on(edge, first_way):
    pairs = []
    for i in range(IFG_COUNT):
        way = first_way if i % 2 == 0 else -first_way
        for b in range(BAND_COUNT):
            if 0 <= b + way < BAND_COUNT:
                pairs.append((i * BAND_COUNT + b, i * BAND_COUNT + b + way))
    return lax.ppermute(edge, ("ifg", "band"), pairs)


def edge_weights(start, count, total):
    offsets = jnp.arange(-RIM_WIDTH, RIM_WIDTH + 1, dtype=jnp.int32)
    places = start + jnp.arange(count, dtype=jnp.int32)[:, None] + offsets[None, :]
    inside = ((places >= 0) & (places < total)).astype(jnp.float32)
    return jnp.sum(inside * tap(offsets.astype(jnp.float32))[None, :], axis=1)


def body(unwrapped, component_mask, date_pairs):
    blocks = pack(unwrapped.transpose(1, 0, 2), component_mask.transpose(1, 0, 2))
    data = lax.all_to_all(blocks, "ifg", split_axis=0, concat_axis=0, tiled=True)
    row_norm = edge_weights(lax.axis_index("band") * ROWS, ROWS, ROWS * BAND_COUNT)
    row_scale = jnp.broadcast_to((1.0 / row_norm)[:, None], (ROWS, 128))
    column_norm = edge_weights(lax.axis_index("ifg") * COLS, COLS, COLS * IFG_COUNT)
    pairs = date_pairs.T
    ordered = pairs.reshape(2, IFG_COUNT, GROUPS, GROUP).transpose(0, 2, 1, 3).reshape(2, IFGS)
    column_scale = jnp.broadcast_to((1.0 / column_norm)[:, None], (COLS, 128))
    solve, *filtered = operators(pairs)
    sums, smooth, edge_a, edge_b = project_varying(ordered, data, filtered, column_scale)
    edge_a, edge_b = pass_on(edge_a, 1), pass_on(edge_b, -1)
    series, partial = project_series(row_scale, solve, sums, smooth)
    corrected = correct(row_scale, partial, edge_a, edge_b)
    return series.transpose(2, 0, 1), corrected.transpose(2, 0, 1)


def solution(mesh):
    placed = (P("ifg", "band", None), P("ifg", "band", None), P())
    return jax.shard_map(
        body,
        mesh=mesh,
        in_specs=placed,
        out_specs=(P(None, "band", "ifg"), P(None, "band", "ifg")),
        check_vma=False,
    )
```
